32 devices in a mesh: tok: 4 (over z), row: 4 (over y, x), col: 2 (over core).
Axes of the slice: x: 2, y: 2, z: 4, core: 2. Of those that a mesh axis runs over, the one named last changes fastest.
Arguments:
- tokens: bfloat16 [16384, 768], P(('tok', 'row'), 'col'), may hold values from -6 to 6
- cotangent: bfloat16 [16384, 768], P(('tok', 'row'), 'col'), may hold values from -6 to 6
- lengths: int32 [4, 4], P('tok'), may hold values from 1 to 64, 128 in all within a row
- dealing: int32 [512], replicated, may hold values from 0 to 511, as said below
- project_in: bfloat16 [768, 3, 768], P('col', None, 'row'), may hold values from -0.21875 to 0.21875
- project_bias: bfloat16 [2, 768], P(None, 'row'), may hold values from -1.1953125 to 1.1953125
- project_out: bfloat16 [768, 768], P('row', 'col'), may hold values from -4 to 4
- output_bias: bfloat16 [768], P('col'), may hold values from -1.1953125 to 1.1953125
- first_gain: bfloat16 [768], P('col'), may hold values from 0.5 to 1.5
- first_shift: bfloat16 [768], P('col'), may hold values from -1.1953125 to 1.1953125
- up_weight: bfloat16 [768, 3072], P('col', 'row'), may hold values from -0.21875 to 0.21875
- up_bias: bfloat16 [3072], P('row'), may hold values from -1.1953125 to 1.1953125
- down_weight: bfloat16 [3072, 768], P('row', 'col'), may hold values from -0.109375 to 0.109375
- down_bias: bfloat16 [768], P('col'), may hold values from -1.1953125 to 1.1953125
- second_gain: bfloat16 [768], P('col'), may hold values from 0.5 to 1.5
- second_shift: bfloat16 [768], P('col'), may hold values from -1.1953125 to 1.1953125
Outputs:
- output: bfloat16 [16384, 768], P(('tok', 'row'), 'col')
- input_grad: bfloat16 [16384, 768], P(('tok', 'row'), 'col')
- project_in_grad: float32 [768, 3, 768], P('col', None, 'row')
- project_bias_grad: float32 [2, 768], P(None, 'row')
- project_out_grad: float32 [768, 768], P('row', 'col')
- output_bias_grad: float32 [768], P('col')
- first_gain_grad: float32 [768], P('col')
- first_shift_grad: float32 [768], P('col')
- up_weight_grad: float32 [768, 3072], P('col', 'row')
- up_bias_grad: float32 [3072], P('row')
- down_weight_grad: float32 [3072, 768], P('row', 'col')
- down_bias_grad: float32 [768], P('col')
- second_gain_grad: float32 [768], P('col')
- second_shift_grad: float32 [768], P('col')
The draws below stay inside these ranges and needn't reach their ends.
Inputs may be any that keep to these rules, and one draw needn't show every extreme that they name: lengths[g] are the lengths, counted in blocks of 32 tokens, of group g's 4 sequences in the dealt order; every row sums to 128, and its largest is 64. dealing is a permutation of the blocks. Blocks are numbered in token order, and the blocks in [k * 32, (k + 1) * 32) form shard k, with row index k % 4 and group k // 4. A block keeps its row index: p and dealing[p] lie in shards of one row index. Each shard of the given order has exactly 8 of its blocks dealt into each group.
All inputs are finite; a program needn't handle non-finite values.
Results may differ from the reference program's by a relative error of at most 0.017.
Values may be sent and summed in bfloat16 or wider, within the bound.
No kernel may reach another device: no remote copies, remote signals or barrier semaphores. Data moves between devices by JAX's collectives and lax.ppermute only.
A program may use at most 192 MiB of HBM per device.

```python
import math
import jax
import jax.numpy as jnp
import numpy as np
from jax import lax

D = 768
HEADS = 12
HEAD = 64
FF = 3072
BLK = 32
SEQS = 4
GROUPS = 4
GRID_ROWS = 4
TOK_GRP = 4096
LONGEST = 2048
TOKENS = 16384
NB_DEV = 32
NBLK = 512


def draw_dealing(key, part):
    per_pair = NB_DEV // GROUPS
    first_key, second_key = jax.random.split(jax.random.fold_in(key, 17))
    shards = GROUPS * GRID_ROWS
    counting = jnp.arange(NB_DEV, dtype=jnp.int32)
    sending = jax.vmap(lambda subkey: jax.random.permutation(subkey, counting))(jax.random.split(first_key, shards)).reshape(GROUPS, GRID_ROWS, NB_DEV)
    placing = jax.vmap(lambda subkey: jax.random.permutation(subkey, counting))(jax.random.split(second_key, shards)).reshape(GROUPS, GRID_ROWS, NB_DEV)
    target_group = sending // per_pair
    source_group = jnp.arange(GROUPS, dtype=jnp.int32)[:, None, None]
    row_ids = jnp.arange(GRID_ROWS, dtype=jnp.int32)[None, :, None]
    slot_ids = counting[None, None, :]
    arrival = source_group * per_pair + sending % per_pair
    landing = placing[target_group, jnp.broadcast_to(row_ids, target_group.shape), arrival]
    target = (target_group * GRID_ROWS + row_ids) * NB_DEV + landing
    source = jnp.broadcast_to((source_group * GRID_ROWS + row_ids) * NB_DEV + slot_ids, target.shape)
    return jnp.zeros((NBLK,), jnp.int32).at[target.reshape(-1)].set(source.reshape(-1))


def block_scale(own_key, extent, cuts, smallest, largest):
    def one(axis_at, shards_of):
        heights = jax.random.uniform(jax.random.fold_in(jax.random.fold_in(own_key, 6), axis_at), (shards_of,), jnp.float32, smallest / len(cuts), largest / len(cuts))
        return jnp.repeat(jnp.exp(heights), extent[axis_at] // shards_of).reshape((-1,) + (1,) * (len(extent) - axis_at - 1))

    level = one(*cuts[0])
    for cut in cuts[1:]:
        level = level * one(*cut)
    return level


def profile(amount, total, bound, lean):
    portions = [(1 << 20) // math.isqrt(standing ** lean) + 1 for standing in range(2, amount + 1)]
    surplus, counts = total - bound - (amount - 1), [1] * (amount - 1)
    while surplus > 0:
        movable = [i for i in range(amount - 1) if counts[i] < bound]
        pool, budget = sum([portions[i] for i in movable]), surplus
        for i in movable:
            extra = min(bound - counts[i], max(1, budget * portions[i] // pool), surplus)
            counts[i] = counts[i] + extra
            surplus = surplus - extra
    return np.array([bound] + counts)


def uneven(rng, number_of, total, reach, slope):
    if number_of == 2:
        one = jax.random.randint(rng, (), max(1, total - reach), min(reach, total - 1) + 1)
        return jnp.stack([one, total - one])
    tallies = jnp.asarray(profile(number_of, total, reach, slope), jnp.int32)
    couples = (number_of - 1) // 2
    source_of, receiver = tallies[1:1 + 2 * couples:2], tallies[2:2 + 2 * couples:2]
    room = jnp.minimum(source_of - 1, reach - receiver)
    shifted = jax.random.randint(jax.random.fold_in(rng, 1), (couples,), 0, 1 << 20) % (room + 1)
    tallies = tallies.at[1:1 + 2 * couples:2].set(source_of - shifted).at[2:2 + 2 * couples:2].set(receiver + shifted)
    return tallies[jax.random.permutation(jax.random.fold_in(rng, 2), number_of)]


def bell_draw(stream_key, shape, deviation, reach, cuts=(), kind=jnp.bfloat16):
    level = block_scale(stream_key, shape, cuts, -0.22, 0.18) if cuts else 1.0
    values = jax.random.normal(stream_key, shape, jnp.float32) * deviation * level
    return jnp.minimum(jnp.maximum(values, -reach), reach).astype(kind)


def setup_inputs(seed: int = 0) -> dict:
    keys = jax.random.split(jax.random.key(seed), 17)
    return {
        "tokens": bell_draw(keys[0], (TOKENS, D), 1.0, 6.0, ((0, 16), (1, 2))),
        "cotangent": bell_draw(keys[1], (TOKENS, D), 1.0, 6.0, ((0, 16), (1, 2))),
        "lengths": jax.vmap(lambda own: uneven(own, SEQS, TOK_GRP // BLK, LONGEST // BLK, 1))(jax.random.split(keys[2], GROUPS)).reshape((GROUPS, SEQS)).astype(jnp.int32),
        "dealing": draw_dealing(jax.random.fold_in(keys[16], 71), 0),
        "project_in": bell_draw(keys[4], (D, 3, D), D ** -0.5, 0.21875, ((0, 2), (2, 4))),
        "project_bias": bell_draw(keys[5], (2, D), 0.2, 1.1953125, ((1, 4),)),
        "project_out": bell_draw(keys[6], (D, D), 2 ** -0.5, 4.0, ((0, 4), (1, 2))),
        "output_bias": bell_draw(keys[7], (D,), 0.2, 1.1953125, ((0, 2),)),
        "first_gain": jnp.clip(1.0 + 0.1 * jax.random.normal(keys[8], (D,), jnp.float32), 0.5, 1.5).astype(jnp.bfloat16),
        "first_shift": bell_draw(keys[9], (D,), 0.2, 1.1953125, ((0, 2),)),
        "up_weight": bell_draw(keys[10], (D, FF), D ** -0.5, 0.21875, ((0, 2), (1, 4))),
        "up_bias": bell_draw(keys[11], (FF,), 0.2, 1.1953125, ((0, 4),)),
        "down_weight": bell_draw(keys[12], (FF, D), FF ** -0.5, 0.109375, ((0, 4), (1, 2))),
        "down_bias": bell_draw(keys[13], (D,), 0.2, 1.1953125, ((0, 2),)),
        "second_gain": jnp.clip(1.0 + 0.1 * jax.random.normal(keys[14], (D,), jnp.float32), 0.5, 1.5).astype(jnp.bfloat16),
        "second_shift": bell_draw(keys[15], (D,), 0.2, 1.1953125, ((0, 2),)),
    }


EPSILON = 1e-12
MASKED = -1000000000.0

@jax.custom_vjp
def low(v):
    return lax.optimization_barrier(v.astype(jnp.bfloat16)).astype(jnp.float32)

@jax.custom_vjp
def low_back(v):
    return v

def low_keep(v):
    return (low(v), None)

def low_pass(kept, grad):
    return (grad,)

def back_keep(v):
    return (v, None)

def back_low(kept, grad):
    return (low(grad),)
low.defvjp(low_keep, low_pass)
low_back.defvjp(back_keep, back_low)

def matmul(factor, operand):
    return jnp.dot(factor, operand, precision=lax.Precision.HIGHEST)

def layer_norm(resid, gain, shift):
    mean_value = lax.optimization_barrier(jnp.mean(resid, axis=-1, keepdims=True))
    centred = resid - mean_value
    variance = lax.optimization_barrier(jnp.mean(centred * centred, axis=-1, keepdims=True))
    return centred * lax.rsqrt(variance + EPSILON) * gain + shift

def block_layer(params, inputs, segment):
    project_in, project_bias, project_out, output_bias, first_gain, first_shift, up_weight, up_bias, down_weight, down_bias, second_gain, second_shift = params
    joined = matmul(inputs, project_in.reshape(D, 3 * D))
    queries = low_back(low(joined[:, :D] + project_bias[0]))
    keys_all = low_back(low(joined[:, D:2 * D]))
    values_all = low_back(low(joined[:, 2 * D:] + project_bias[1]))
    scale = 1.0 / math.sqrt(HEAD)
    key_heads = keys_all.reshape(TOK_GRP, HEADS, HEAD)
    value_heads = values_all.reshape(TOK_GRP, HEADS, HEAD)
    rows_block = min(512, TOK_GRP)
    block_total = TOK_GRP // rows_block

    def attend(pieces):
        query_block, segment_block = pieces
        scores = jnp.einsum('qhd,khd->hqk', query_block, key_heads, precision=lax.Precision.HIGHEST) * scale
        scores = low_back(scores)
        matching = (segment_block[:, None] == segment[None, :])[None]
        scores = jnp.where(matching, scores, MASKED)
        maximum = lax.optimization_barrier(jnp.max(scores, axis=-1, keepdims=True))
        weights = jnp.exp(scores - maximum)
        shares = low(weights / lax.optimization_barrier(jnp.sum(weights, axis=-1, keepdims=True)))
        return jnp.einsum('hqk,khd->qhd', shares, value_heads, precision=lax.Precision.HIGHEST)
    mixed = lax.map(jax.checkpoint(attend), (queries.reshape(block_total, rows_block, HEADS, HEAD), segment.reshape(block_total, rows_block)))
    heads_out = low_back(low(mixed.reshape(TOK_GRP, D)))
    attention = low_back(matmul(heads_out, project_out) + output_bias)
    hidden = layer_norm(inputs + attention, first_gain, first_shift)
    upward = low_back(matmul(low(hidden), up_weight) + up_bias)
    activated = low(jax.nn.gelu(upward, approximate=False))
    downward = low_back(matmul(activated, down_weight) + down_bias)
    return layer_norm(hidden + downward, second_gain, second_shift)

def reference(tokens, cotangent, lengths, dealing, project_in, project_bias, project_out, output_bias, first_gain, first_shift, up_weight, up_bias, down_weight, down_bias, second_gain, second_shift):
    params = tuple((item.astype(jnp.float32) for item in (project_in, project_bias, project_out, output_bias, first_gain, first_shift, up_weight, up_bias, down_weight, down_bias, second_gain, second_shift)))
    dealt_x = tokens.reshape(NBLK, BLK, D)[dealing].reshape(GROUPS, TOK_GRP, D).astype(jnp.float32)
    dealt_dy = cotangent.reshape(NBLK, BLK, D)[dealing].reshape(GROUPS, TOK_GRP, D).astype(jnp.float32)
    ends = jnp.cumsum(lengths, axis=1).astype(jnp.int32) * BLK
    positions = jnp.arange(TOK_GRP, dtype=jnp.int32)

    def one_group(running, inputs):
        group_x, group_dy, group_ends = inputs
        segment = lax.optimization_barrier(jnp.sum((positions[:, None] >= group_ends[None, :]).astype(jnp.int32), axis=1)).astype(jnp.int32)
        result, pullback = jax.vjp(lambda weights_all, layer_in: block_layer(weights_all, layer_in, segment), params, group_x)
        weight_grads, input_grads = pullback(group_dy)
        running = jax.tree.map(jnp.add, running, weight_grads)
        return (running, (result, input_grads))
    zeros = tuple((jnp.zeros_like(item) for item in params))
    totals, (results, input_grads) = lax.scan(one_group, zeros, (dealt_x, dealt_dy, ends))
    inverse = jnp.zeros((NBLK,), jnp.int32).at[dealing].set(jnp.arange(NBLK, dtype=jnp.int32))
    output = results.reshape(NBLK, BLK, D)[inverse].reshape(TOKENS, D).astype(jnp.bfloat16)
    input_grad = input_grads.reshape(NBLK, BLK, D)[inverse].reshape(TOKENS, D).astype(jnp.bfloat16)
    return (output, input_grad, totals[0], totals[1], totals[2], totals[3], totals[4], totals[5], totals[6], totals[7], totals[8], totals[9], totals[10], totals[11])
```

```python
from functools import partial

import jax
import jax.numpy as jnp
from jax import lax
from jax.experimental import pallas as pl
from jax.experimental.pallas import tpu as pltpu
from jax.sharding import PartitionSpec as P

HEAD = 64
LANES = 128
EPSILON = 1e-12
OFF = -1000000000.0
BF = jnp.bfloat16
F32 = jnp.float32
VMEM_LIMIT = 60 * 1024 * 1024


def nn(a, b):
    return lax.dot_general(a, b, (((1,), (0,)), ((), ())), preferred_element_type=F32)


def nt(a, b):
    return lax.dot_general(a, b, (((1,), (1,)), ((), ())), preferred_element_type=F32)


def tn(a, b):
    return lax.dot_general(a, b, (((0,), (0,)), ((), ())), preferred_element_type=F32)


def call(kernel, outs, spaces, scratch=(), flops=0, moved=0):
    memory = {"s": pltpu.SMEM, "v": pltpu.VMEM}
    return pl.pallas_call(
        kernel,
        out_shape=[jax.ShapeDtypeStruct(shape, dtype) for shape, dtype in outs],
        in_specs=[pl.BlockSpec(memory_space=memory[s]) for s in spaces],
        out_specs=[pl.BlockSpec(memory_space=pltpu.VMEM) for _ in outs],
        scratch_shapes=list(scratch),
        compiler_params=pltpu.CompilerParams(vmem_limit_bytes=VMEM_LIMIT),
        cost_estimate=pl.CostEstimate(flops=flops, bytes_accessed=moved, transcendentals=0),
    )


def rows_at(block, size):
    return pl.ds(pl.multiple_of(block * size, size), size)


def send_kernel(sizes, deal, where, x, *outs):
    groups, grid_rows, count, block = sizes
    g, r = where[0], where[1]
    mine = g * grid_rows + r
    for d in range(groups):
        base = (lax.rem(g + d, groups) * grid_rows + r) * count

        def step(j, rank):
            source = deal[base + j]
            hit = lax.div(source, count) == mine

            @pl.when(hit)
            def _():
                outs[d][rows_at(rank, block), :] = x[rows_at(lax.rem(source, count), block), :]

            return rank + hit.astype(jnp.int32)

        lax.fori_loop(0, count, step, jnp.int32(0))


def final_kernel(sizes, deal, where, *refs):
    groups, grid_rows, count, block = sizes
    pieces, out = refs[:groups], refs[groups]
    g, r = where[0], where[1]
    mine = g * grid_rows + r
    for d in range(groups):
        base = (lax.rem(g + groups - d, groups) * grid_rows + r) * count

        def step(j, rank):
            source = deal[base + j]
            hit = lax.div(source, count) == mine

            @pl.when(hit)
            def _():
                out[rows_at(lax.rem(source, count), block), :] = pieces[d][rows_at(rank, block), :]

            return rank + hit.astype(jnp.int32)

        lax.fori_loop(0, count, step, jnp.int32(0))


def home_of(j, run, c):
    turn = lax.div(j, run)
    return lax.rem(turn, 2), lax.div(turn, 2) * run + lax.rem(j, run)


def arrive_kernel(sizes, run, deal, where, *refs):
    groups, grid_rows, count, block = sizes
    pieces, own, other, ranks = refs[:groups], refs[groups], refs[groups + 1], refs[groups + 2]
    g, r, c = where[0], where[1], where[2]
    base = (g * grid_rows + r) * count
    for d in range(groups):
        origin = lax.rem(g + groups - d, groups)

        def step(j, rank):
            hit = lax.div(deal[base + j], grid_rows * count) == origin

            @pl.when(hit)
            def _():
                core, place = home_of(j, run, c)
                rows = pieces[d][rows_at(rank, block), :]

                @pl.when(core == c)
                def _():
                    own[rows_at(place, block), :] = rows

                @pl.when(core != c)
                def _():
                    other[rows_at(place, block), :] = rows

            return rank + hit.astype(jnp.int32)

        lax.fori_loop(0, count, step, jnp.int32(0))


def return_kernel(sizes, run, deal, where, own, other, *outs):
    groups, grid_rows, count, block = sizes
    g, r, c = where[0], where[1], where[2]
    base = (g * grid_rows + r) * count
    for d in range(groups):
        origin = lax.rem(g + d, groups)

        def step(j, rank):
            hit = lax.div(deal[base + j], grid_rows * count) == origin

            @pl.when(hit)
            def _():
                core, place = home_of(j, run, c)

                @pl.when(core == c)
                def _():
                    outs[d][rows_at(rank, block), :] = own[rows_at(place, block), :]

                @pl.when(core != c)
                def _():
                    outs[d][rows_at(rank, block), :] = other[rows_at(place, block), :]

            return rank + hit.astype(jnp.int32)

        lax.fori_loop(0, count, step, jnp.int32(0))


def sequence_ends(lengths, number):
    ends, total = [], jnp.int32(0)
    for s in range(number):
        total = total + lengths[0, s]
        ends.append(total)
    return ends


def sequence_of(ends, block):
    return sum((block >= end).astype(jnp.int32) for end in ends)


def first_of(ends, block):
    start = jnp.int32(0)
    for end in ends:
        start = jnp.where(block >= end, end, start)
    return start


def last_of(ends, block):
    stop = ends[-1]
    for end in reversed(ends):
        stop = jnp.where(block < end, end, stop)
    return stop


def thirds(v):
    one = v.astype(BF)
    rest = v - one.astype(F32)
    two = rest.astype(BF)
    three = (rest - two.astype(F32)).astype(BF)
    return one.astype(F32), two.astype(F32), three.astype(F32)


def attend_kernel(sizes, chunk_blocks, heads, seqs, run, deal, where, lengths, *refs):
    groups, grid_rows, count, block = sizes
    chunks = len(chunk_blocks)
    pieces = refs[: chunks * grid_rows * 2]
    weights = refs[chunks * grid_rows * 2 : chunks * grid_rows * 2 + 2]
    bias = refs[chunks * grid_rows * 2 + 2]
    outs = refs[chunks * grid_rows * 2 + 3 :]
    q_ref, k_ref, v_ref, o_ref, xq_ref, own_ref = outs[:6]
    mixed = outs[6 : 6 + grid_rows]
    place, tally = outs[6 + grid_rows :]
    g, r, c = where[0], where[1], where[2]
    ends = sequence_ends(lengths, seqs)
    per_pair = count // groups
    for k in range(grid_rows):
        row = r ^ k
        for d in range(groups):
            tally[d] = 0

        def step(j, carry):
            origin = lax.div(deal[(g * grid_rows + row) * count + j], grid_rows * count)
            d = lax.rem(g - origin + groups, groups)
            rank = tally[d]
            tally[d] = rank + 1
            place[k, d * per_pair + rank] = row * count + j
            return carry

        lax.fori_loop(0, count, step, jnp.int32(0))
    lane = lax.broadcasted_iota(jnp.int32, (block, HEAD), 1)
    ones_v = jnp.where(lane < 3, 1.0, 0.0)
    tail_k = (lane >= seqs) & (lane < seqs + 3)
    w0, w1 = weights[0][...], weights[1][...]
    q_bias, v_bias = bias[0:1, :].astype(F32), bias[1:2, :].astype(F32)
    unit = 8
    start = 0
    for chunk, blocks in enumerate(chunk_blocks):
        for k in range(grid_rows):
            x0, x1 = pieces[(chunk * grid_rows + k) * 2], pieces[(chunk * grid_rows + k) * 2 + 1]
            for part in range(blocks // unit):
                span = slice(part * unit * block, (part + 1) * unit * block)
                joined = nt(x0[span, :], w0) + nt(x1[span, :], w1)
                for b in range(unit):
                    at = place[k, start + part * unit + b]
                    seg = sequence_of(ends, at)
                    core, local = home_of(at, run, c)
                    inside = slice(b * block, (b + 1) * block)
                    key_tail = jnp.where((lane == seg) | tail_k, 1.0, 0.0)
                    for h in range(heads):
                        left = h * 3 * HEAD
                        key = joined[inside, left + HEAD : left + 2 * HEAD]
                        value = joined[inside, left + 2 * HEAD : left + 3 * HEAD] + v_bias[:, h * HEAD : (h + 1) * HEAD]
                        k_ref[h, rows_at(at, block), :] = jnp.concatenate([key, key_tail], axis=1).astype(BF)
                        v_ref[h, rows_at(at, block), :] = jnp.concatenate([value, ones_v], axis=1).astype(BF)

                    @pl.when(core == c)
                    def _():
                        query_tail = jnp.where((lane < seqs) & (lane != seg), OFF, 0.0)
                        for h in range(heads):
                            left = h * 3 * HEAD
                            query = joined[inside, left : left + HEAD] + q_bias[:, h * HEAD : (h + 1) * HEAD]
                            query = query.astype(BF).astype(F32) * (HEAD**-0.5)
                            q_ref[h, rows_at(local, block), :] = jnp.concatenate([query, query_tail], axis=1).astype(BF)
                        here = slice((part * unit + b) * block, (part * unit + b + 1) * block)
                        xq_ref[rows_at(local, block), : x0.shape[1]] = x0[here, :]
                        xq_ref[rows_at(local, block), x0.shape[1] :] = x1[here, :]

        start += blocks
    rows = run * block
    local_runs = q_ref.shape[1] // rows
    shard_runs = local_runs // grid_rows
    own_ref[...] = xq_ref[rows_at(r, rows * shard_runs), :]
    wide = 2
    lane_q = lax.broadcasted_iota(jnp.int32, (rows, LANES), 1)
    for h in range(heads):

        def one_run(i, carry):
            first = i * 2 * run + c * run
            low = lax.div(first_of(ends, first), wide * run)
            high = lax.div(last_of(ends, first + run - 1) + wide * run - 1, wide * run)
            query = q_ref[h, rows_at(i, rows), :]

            def keys(j, state):
                top, acc = state
                scores = nt(query, k_ref[h, rows_at(j, wide * rows), :])
                peak = jnp.maximum(top, jnp.max(scores, axis=1, keepdims=True))
                part = jnp.exp(scores - peak).astype(BF)
                acc = acc * jnp.exp(top - peak) + nn(part, v_ref[h, rows_at(j, wide * rows), :])
                return peak, acc

            top, acc = lax.fori_loop(
                low, high, keys, (jnp.full((rows, 1), -3e38, F32), jnp.zeros((rows, LANES), F32))
            )
            total = acc[:, HEAD : HEAD + 1]
            o_ref[h, rows_at(i, rows), :] = (acc[:, :HEAD] / total).astype(BF)
            terms = thirds(top + jnp.log(total))
            kept = query.astype(F32)
            for t, term in enumerate(terms):
                kept = jnp.where(lane_q == HEAD + seqs + t, -term, kept)
            q_ref[h, rows_at(i, rows), :] = kept.astype(BF)
            return carry

        lax.fori_loop(0, local_runs, one_run, jnp.int32(0))
    for k in range(grid_rows):
        cells = [
            o_ref[h, rows_at((r ^ k) * shard_runs + half, rows), :] for half in range(shard_runs) for h in range(heads)
        ]
        mixed[k][...] = jnp.concatenate(cells, axis=1)


def attend_back_kernel(grid_rows, heads, seqs, run, block, where, lengths, q_ref, k_ref, v_ref, o_ref, *refs):
    grads = refs[:grid_rows]
    dq_ref, own_ref, other_ref, do_ref, acc_ref, key_acc, value_acc = refs[grid_rows:]
    r, c = where[1], where[2]
    ends = sequence_ends(lengths, seqs)
    rows = run * block
    local_runs = q_ref.shape[1] // rows
    shard_runs = local_runs // grid_rows
    lane = lax.broadcasted_iota(jnp.int32, (rows, HEAD), 1)
    for k in range(grid_rows):
        for half in range(shard_runs):
            at = rows_at((r ^ k) * shard_runs + half, rows)
            for h in range(heads):
                left = (half * heads + h) * HEAD
                grad = grads[k][:, left : left + HEAD].astype(F32)
                centre = jnp.sum(grad * o_ref[h, at, :].astype(F32), axis=1, keepdims=True)
                tail = jnp.zeros((rows, HEAD), F32)
                for t, term in enumerate(thirds(centre)):
                    tail = jnp.where(lane == t, -term, tail)
                do_ref[h, at, :] = jnp.concatenate([grad, tail], axis=1).astype(BF)
    for h in range(heads):
        acc_ref[...] = jnp.zeros_like(acc_ref)

        def key_run(i, core):
            low = first_of(ends, i * run)
            high = last_of(ends, i * run + run - 1)
            key = k_ref[h, rows_at(i, rows), :]
            value = v_ref[h, rows_at(i, rows), :]
            key_acc[...] = jnp.zeros_like(key_acc)
            value_acc[...] = jnp.zeros_like(value_acc)

            def query_run(j, carry):
                query = q_ref[h, rows_at(j, rows), :]
                grad = do_ref[h, rows_at(j, rows), :]
                shares = jnp.exp(nt(key, query))
                score_grads = (shares * nt(value, grad)).astype(BF)
                value_acc[...] += nn(shares.astype(BF), grad)
                key_acc[...] += nn(score_grads, query)
                acc_ref[rows_at(j, rows), :] += tn(score_grads, key)
                return carry

            lax.fori_loop(
                lax.div(low - c * run + run, 2 * run), lax.div(high - c * run + 2 * run - 1, 2 * run), query_run, jnp.int32(0)
            )
            return jnp.concatenate([key_acc[:, :HEAD], value_acc[:, :HEAD]], axis=1)

        def pair(i, carry):
            own_ref[h, rows_at(i, rows), :] = key_run(2 * i + c, 0)
            other_ref[h, rows_at(i, rows), :] = key_run(2 * i + 1 - c, 1).astype(BF)
            return carry

        lax.fori_loop(0, local_runs, pair, jnp.int32(0))
        dq_ref[h, :, :] = (acc_ref[:, :HEAD] * (HEAD**-0.5)).astype(BF)


def join_kernel(grid_rows, heads, where, dq_ref, own_ref, got_ref, *refs):
    pieces, joined = refs[:grid_rows], refs[grid_rows]
    r = where[1]
    rows = pieces[0].shape[0] // heads
    shard_runs = pieces[0].shape[1] // (3 * HEAD)
    for k in range(grid_rows):
        for h in range(heads):
            cells = []
            for half in range(shard_runs):
                at = rows_at((r ^ k) * shard_runs + half, rows)
                both = (own_ref[h, at, :] + got_ref[h, at, :].astype(F32)).astype(BF)
                cells += [dq_ref[h, at, :], both]
                joined[at, h * 3 * HEAD : (h + 1) * 3 * HEAD] = jnp.concatenate([dq_ref[h, at, :], both], axis=1)
            pieces[k][h * rows : (h + 1) * rows, :] = jnp.concatenate(cells, axis=1)


def project_in_grad_kernel(joined, xq, own, other):
    half = own.shape[1]
    wide = joined.shape[1]
    total = jnp.sum(joined[...].astype(F32), axis=0, keepdims=True)
    pad = jnp.zeros((1, 2 * half - wide), F32)
    total = jnp.concatenate([total, pad], axis=1)
    below = own.shape[0] - wide
    sums = jnp.concatenate([total[:, :half], total[:, half:], jnp.zeros((below - 2, half), F32)], axis=0).astype(BF)
    own[:wide, :] = tn(joined[...], xq[:, :half]).astype(BF)
    other[:wide, :] = tn(joined[...], xq[:, half:]).astype(BF)
    own[wide:, :] = sums
    other[wide:, :] = sums


def middle_kernel(plan, grid_rows, where, *refs):
    at = 0

    def take(n):
        nonlocal at
        got = refs[at : at + n]
        at += n
        return got

    mixed = take(grid_rows)
    (x_ref,) = take(1)
    dy = take(2)
    first = take(2 * grid_rows)
    second = take(2 * grid_rows)
    outs = take(2)
    act_ref, up_grad_ref, hidden_ref, down_grad_ref, attn_grad_ref, grad_one_ref = take(6)
    mixed_grad = take(grid_rows)
    (small,) = take(1)
    (slope_ref,) = take(1)
    half = dy[0].shape[1]
    width = 2 * half
    inner = mixed[0].shape[1] // 2
    rows = mixed[0].shape[0]
    r, c = where[1], where[2]
    small[...] = jnp.zeros_like(small)

    def vector(index):
        row = plan["vectors"] + index
        return jnp.concatenate([second[0][row : row + 1, :], second[1][row : row + 1, :]], axis=1).astype(F32)

    output_bias, first_gain, first_shift, down_bias, second_gain, second_shift = (vector(i) for i in range(6))

    def mean(v):
        return jnp.sum(v, axis=1, keepdims=True) / width

    def norm(v):
        centred = v - mean(v)
        inverse = lax.rsqrt(mean(centred * centred) + EPSILON)
        return centred * inverse, inverse

    def norm_back(v, normed, inverse):
        return inverse * (v - mean(v) - normed * mean(v * normed))

    def total(v):
        return jnp.sum(v, axis=0, keepdims=True)

    def keep(row, v):
        small[row : row + 1, :] += v

    for part in range(2):
        span = slice(part * rows, (part + 1) * rows)
        lanes = slice(part * inner, (part + 1) * inner)
        parts = []
        for j in range(2):
            parts.append(sum(nn(mixed[k][:, lanes], first[2 * k + j][plan["out"], :]) for k in range(grid_rows)))
        attention = jnp.concatenate(parts, axis=1) + output_bias
        normed_one, inverse_one = norm(x_ref[span, :].astype(F32) + attention)
        hidden = normed_one * first_gain + first_shift
        low = hidden.astype(BF)
        hidden_ref[span, :] = low
        downs = [jnp.zeros((rows, half), F32), jnp.zeros((rows, half), F32)]
        for k in range(grid_rows):
            for u in range(2):
                cols = slice((2 * k + u) * half, (2 * k + u + 1) * half)
                up_rows = plan["up"][u]
                upward = nn(low[:, :half], first[2 * k][up_rows, :]) + nn(low[:, half:], first[2 * k + 1][up_rows, :])
                upward = upward + first[2 * k][plan["up_bias"] + u : plan["up_bias"] + u + 1, :].astype(F32)
                bell = (1.0 + lax.erf(upward * (2.0**-0.5))) * 0.5
                slope_ref[:, cols] = bell + upward * jnp.exp(upward * upward * -0.5) * 0.3989422804014327
                act = (upward * bell).astype(BF)
                act_ref[span, cols] = act
                down_rows = plan["down"][u]
                for j in range(2):
                    downs[j] = downs[j] + nn(act, second[2 * k + j][down_rows, :])
        downward = jnp.concatenate(downs, axis=1) + down_bias
        normed_two, inverse_two = norm(hidden + downward)
        final = (normed_two * second_gain + second_shift).astype(BF)
        outs[0][span, :] = final[:, :half]
        outs[1][span, :] = final[:, half:]
        grad_out = jnp.concatenate([dy[0][span, :], dy[1][span, :]], axis=1).astype(F32)
        keep(0, total(grad_out * normed_two))
        keep(1, total(grad_out))
        grad_two = norm_back(grad_out * second_gain, normed_two, inverse_two)
        down_grad = grad_two.astype(BF)
        down_grad_ref[span, :] = down_grad
        keep(4, total(down_grad.astype(F32)))
        grads = [grad_two[:, :half], grad_two[:, half:]]
        for k in range(grid_rows):
            for u in range(2):
                cols = slice((2 * k + u) * half, (2 * k + u + 1) * half)
                up_rows, down_rows = plan["up"][u], plan["down"][u]
                act_grad = nt(down_grad[:, :half], second[2 * k][down_rows, :]) + nt(
                    down_grad[:, half:], second[2 * k + 1][down_rows, :]
                )
                up_grad = (act_grad * slope_ref[:, cols]).astype(BF)
                up_grad_ref[span, cols] = up_grad
                row = pl.ds(8 + (r ^ k), 1)
                small[row, u * half : (u + 1) * half] += total(up_grad.astype(F32))
                for j in range(2):
                    grads[j] = grads[j] + nt(up_grad, first[2 * k + j][up_rows, :])
        grad_hidden = jnp.concatenate(grads, axis=1)
        keep(2, total(grad_hidden * normed_one))
        keep(3, total(grad_hidden))
        grad_one = norm_back(grad_hidden * first_gain, normed_one, inverse_one)
        grad_one_ref[span, :] = grad_one
        attn_grad = grad_one.astype(BF)
        attn_grad_ref[span, :] = attn_grad
        keep(5, total(attn_grad.astype(F32)))
        for k in range(grid_rows):
            back = nt(attn_grad[:, :half], first[2 * k][plan["out"], :]) + nt(
                attn_grad[:, half:], first[2 * k + 1][plan["out"], :]
            )
            mixed_grad[k][:, lanes] = back.astype(BF)
    sums = small[:8, :]
    small[:8, :] = jnp.where(c == 0, sums, jnp.concatenate([sums[:, half:], sums[:, :half]], axis=1))


def middle_grad_kernel(plan, grid_rows, *refs):
    mixed = refs[:grid_rows]
    act, up_grad, hidden, down_grad, attn_grad = refs[grid_rows : grid_rows + 5]
    first, second = refs[grid_rows + 5 : grid_rows + 7], refs[grid_rows + 7 : grid_rows + 9]
    half = hidden.shape[1] // 2
    rows, inner = mixed[0].shape[0], mixed[0].shape[1] // 2
    for j in range(2):
        side = slice(j * half, (j + 1) * half)
        for place, k in enumerate(plan["second_order"]):
            for u in range(2):
                cols = slice((2 * k + u) * half, (2 * k + u + 1) * half)
                second[j][place, plan["down"][u], :] = tn(act[:, cols], down_grad[:, side]).astype(BF)
        for place, k in enumerate(plan["first_order"]):
            for u in range(2):
                cols = slice((2 * k + u) * half, (2 * k + u + 1) * half)
                first[j][place, plan["up"][u], :] = tn(hidden[:, side], up_grad[:, cols]).astype(BF)
            back = tn(mixed[k][:, :inner], attn_grad[:rows, side]) + tn(mixed[k][:, inner:], attn_grad[rows:, side])
            first[j][place, plan["out"], :] = back.astype(BF)


def input_grad_kernel(plan, grid_rows, heads, *refs):
    pieces = refs[:grid_rows]
    second = refs[grid_rows : 3 * grid_rows]
    grad_one, own, other = refs[3 * grid_rows :]
    half = own.shape[1]
    rows = pieces[0].shape[0] // heads
    wide = 3 * HEAD
    for part in range(2):
        span = slice(part * rows, (part + 1) * rows)
        for j, out in enumerate((own, other)):
            total = grad_one[span, j * half : (j + 1) * half]
            for k in range(grid_rows):
                for h in range(heads):
                    top = plan["join"] + h * wide
                    total = total + nn(
                        pieces[k][h * rows : (h + 1) * rows, part * wide : (part + 1) * wide],
                        second[2 * k + j][top : top + wide, :],
                    )
            out[span, :] = total.astype(BF)


def shift(array, axis, to):
    return lax.ppermute(array, axis, [(i, to(i)) for i in range(lax.axis_size(axis))])


def to_row(array, k):
    return shift(array, "row", lambda i: i ^ k)


def to_col(array):
    return shift(array, "col", lambda i: 1 - i)


def after(array, *earlier):
    return lax.optimization_barrier((array, *earlier))[0]


def gather_row(array, turn):
    near, side = to_row(array, 1), to_row(array, 2)
    far = to_row(near, 2) if turn == 0 else to_row(side, 1)
    return [array, near, side, far]


def add(*arrays):
    return sum(a.astype(F32) for a in arrays).astype(BF)


def reduce_row(own, got, turn):
    first, then = (1, 2) if turn == 0 else (2, 1)
    came = to_row(add(own[2:], got[2:]), first)
    last = to_row(add(own[1], got[1], came[1]), then)
    return add(own[0], got[0], came[0], last)


def reduce_groups(array, group):
    if lax.axis_size("tok") != 4:
        return lax.psum(array, "tok")
    side = (group ^ (group >> 1)) & 1
    middle = array.shape[0] // 2
    low, high = array[:middle], array[middle:]
    half = add(jnp.where(side == 0, low, high), shift(jnp.where(side == 0, high, low), "tok", lambda i: i ^ 1))
    half = add(half, shift(half, "tok", lambda i: i ^ 3))
    rest = shift(half, "tok", lambda i: i ^ 1)
    return jnp.concatenate([jnp.where(side == 0, half, rest), jnp.where(side == 0, rest, half)], axis=0)


def local(
    tokens,
    cotangent,
    lengths,
    dealing,
    project_in,
    project_bias,
    project_out,
    output_bias,
    first_gain,
    first_shift,
    up_weight,
    up_bias,
    down_weight,
    down_bias,
    second_gain,
    second_shift,
):
    groups, grid_rows = lax.axis_size("tok"), lax.axis_size("row")
    group, row, col = lax.axis_index("tok"), lax.axis_index("row"), lax.axis_index("col")
    where = jnp.stack([group, row, col]).astype(jnp.int32)
    shard_rows, half = tokens.shape
    width = 2 * half
    count = dealing.shape[0] // (groups * grid_rows)
    block = shard_rows // count
    sizes = (groups, grid_rows, count, block)
    seqs = lengths.shape[1]
    inner = project_bias.shape[1]
    heads = inner // HEAD
    hidden_part = up_weight.shape[1]
    run = count // 4
    rows = run * block
    own_rows = shard_rows // 2
    half_rows = own_rows * grid_rows
    wide = 3 * inner
    piece = (shard_rows // groups, half)
    shard = (shard_rows, half)

    def exchange(pieces):
        return [shift(p, "tok", lambda i, d=d: (i + d) % groups) if d else p for d, p in enumerate(pieces)]

    def send(array):
        return exchange(call(partial(send_kernel, sizes), [(piece, BF)] * groups, "ssv")(dealing, where, array))

    def send_back(own, other):
        pieces = call(partial(return_kernel, sizes, run), [(piece, BF)] * groups, "ssvv")(dealing, where, own, other)
        got = exchange(pieces)
        return call(partial(final_kernel, sizes), [(shard, BF)], "ss" + "v" * groups)(dealing, where, *got)[0]

    joined_weight = (
        project_in.transpose(1, 2, 0).reshape(3, heads, HEAD, half).transpose(1, 0, 2, 3).reshape(wide, half)
    )
    vectors = jnp.stack([output_bias, first_gain, first_shift, down_bias, second_gain, second_shift])
    up_bias_rows = up_bias.reshape(2, half)
    first_weights = jnp.concatenate(
        [up_weight[:, :half], up_weight[:, half:], project_out, jnp.pad(up_bias_rows, ((0, 14), (0, 0)))], axis=0
    )
    second_weights = jnp.concatenate([down_weight, joined_weight, jnp.pad(vectors, ((0, 10), (0, 0)))], axis=0)
    plan = {
        "up": (slice(0, half), slice(half, 2 * half)),
        "out": slice(2 * half, 2 * half + inner),
        "up_bias": 2 * half + inner,
        "down": (slice(0, half), slice(half, 2 * half)),
        "join": hidden_part,
        "vectors": hidden_part + wide,
        "first_order": (0, 2, 1, 3),
        "second_order": (0, 1, 2, 3),
    }

    got = send(tokens)
    if groups == 4:
        chunks, chunk_blocks = got, [count // groups] * groups
    else:
        chunks, chunk_blocks = [jnp.concatenate(got, axis=0)], [count]
    pieces = []
    for turn, chunk in enumerate(chunks):
        for part in gather_row(chunk, turn % 2):
            pieces += [part, to_col(part)]
    q, k, v, mixed_own, xq, x_own, *mixed = call(
        partial(attend_kernel, sizes, chunk_blocks, heads, seqs, run),
        [
            ((heads, half_rows, LANES), BF),
            ((heads, 2 * half_rows, LANES), BF),
            ((heads, 2 * half_rows, LANES), BF),
            ((heads, half_rows, HEAD), BF),
            ((half_rows, width), BF),
            ((own_rows, width), BF),
        ]
        + [((rows, 2 * inner), BF)] * grid_rows,
        "sss" + "v" * (len(pieces) + 3),
        [pltpu.SMEM((grid_rows, count), jnp.int32), pltpu.SMEM((groups,), jnp.int32)],
    )(dealing, where, lengths, *pieces, joined_weight, to_col(joined_weight), project_bias)

    dy_got = send(after(cotangent, *got))
    dy_own, dy_other = call(
        partial(arrive_kernel, sizes, run), [((own_rows, half), BF)] * 2, "ss" + "v" * groups,
        [pltpu.SMEM((groups,), jnp.int32)],
    )(dealing, where, *dy_got)
    dy = [dy_own, to_col(dy_other)]

    firsts, seconds = [], []
    for part in gather_row(first_weights, 0):
        firsts += [part, to_col(part)]
    for part in gather_row(second_weights, 1):
        seconds += [part, to_col(part)]

    mixed_got = [to_row(m, i) if i else m for i, m in enumerate(mixed)]
    hidden_all = grid_rows * hidden_part
    out0, out1, act, up_grad, hidden, down_grad, attn_grad, grad_one, *rest = call(
        partial(middle_kernel, plan, grid_rows),
        [
            ((own_rows, half), BF),
            ((own_rows, half), BF),
            ((own_rows, hidden_all), BF),
            ((own_rows, hidden_all), BF),
            ((own_rows, width), BF),
            ((own_rows, width), BF),
            ((own_rows, width), BF),
            ((own_rows, width), F32),
        ]
        + [((rows, 2 * inner), BF)] * grid_rows
        + [((8 + 8, width), F32)],
        "s" + "v" * (grid_rows + 3 + 4 * grid_rows),
        [pltpu.VMEM((rows, hidden_all), F32)],
    )(where, *mixed_got, x_own, *dy, *firsts, *seconds)
    mixed_grad, small = rest[:grid_rows], rest[grid_rows]
    mixed_grad_got = [to_row(m, i) if i else m for i, m in enumerate(mixed_grad)]
    small = lax.psum(small, ("tok", "row", "col"))

    first_rows = 2 * half + inner
    first_own, first_other, second_own, second_other = call(
        partial(middle_grad_kernel, plan, grid_rows),
        [((grid_rows, first_rows, half), BF)] * 2 + [((grid_rows, hidden_part, half), BF)] * 2,
        "v" * (grid_rows + 5),
    )(*mixed_got, act, up_grad, hidden, down_grad, attn_grad)
    first_sum = reduce_groups(reduce_row(first_own, to_col(first_other), 0), group)
    second_sum = reduce_groups(reduce_row(second_own, to_col(second_other), 1), group)

    output = send_back(out0, to_col(out1))

    dq, kv_own, kv_other = call(
        partial(attend_back_kernel, grid_rows, heads, seqs, run, block),
        [
            ((heads, half_rows, HEAD), BF),
            ((heads, half_rows, LANES), F32),
            ((heads, half_rows, LANES), BF),
        ],
        "ss" + "v" * (4 + grid_rows),
        [
            pltpu.VMEM((heads, half_rows, LANES), BF),
            pltpu.VMEM((half_rows, LANES), F32),
            pltpu.VMEM((rows, LANES), F32),
            pltpu.VMEM((rows, LANES), F32),
        ],
    )(where, lengths, q, k, v, mixed_own, *mixed_grad_got)
    *joined_pieces, joined = call(
        partial(join_kernel, grid_rows, heads),
        [((heads * rows, 2 * 3 * HEAD), BF)] * grid_rows + [((half_rows, wide), BF)],
        "svvv",
    )(where, dq, kv_own, to_col(kv_other))
    joined_got = [to_row(m, i) if i else m for i, m in enumerate(joined_pieces)]
    in_own, in_other = call(project_in_grad_kernel, [((wide + 32, half), BF)] * 2, "vv")(joined, xq)
    in_sum = reduce_groups(add(in_own, to_col(in_other)), group)
    dx_own, dx_other = call(
        partial(input_grad_kernel, plan, grid_rows, heads),
        [((own_rows, half), BF)] * 2,
        "v" * (3 * grid_rows + 1),
    )(*joined_got, *seconds, grad_one)
    input_grad = send_back(dx_own, to_col(dx_other))

    project_in_grad = (
        in_sum[:wide].reshape(heads, 3, HEAD, half).transpose(1, 0, 2, 3).reshape(3, inner, half).transpose(2, 0, 1)
    )
    sums = in_sum[wide : wide + 2].reshape(2 * half)[:wide].reshape(heads, 3, HEAD)
    project_bias_grad = jnp.stack([sums[:, 0].reshape(inner), sums[:, 2].reshape(inner)])
    up_bias_grad = lax.dynamic_slice_in_dim(small, 8 + row, 1, 0)[0]
    vector_grads = lax.dynamic_slice_in_dim(small[:8], col * half, half, 1)
    return (
        output,
        input_grad,
        project_in_grad.astype(F32),
        project_bias_grad.astype(F32),
        first_sum[2 * half :].astype(F32),
        vector_grads[5],
        vector_grads[2],
        vector_grads[3],
        jnp.concatenate([first_sum[:half], first_sum[half : 2 * half]], axis=1).astype(F32),
        up_bias_grad,
        second_sum.astype(F32),
        vector_grads[4],
        vector_grads[0],
        vector_grads[1],
    )


def solution(mesh):
    stream, grid = P(("tok", "row"), "col"), P("row", "col")
    joined, mids, cols = P("col", None, "row"), P("col", "row"), P("col")
    in_specs = (
        stream, stream, P("tok", None), P(), joined, P(None, "row"), grid, cols,
        cols, cols, mids, P("row"), grid, cols, cols, cols,
    )
    out_specs = (
        stream, stream, joined, P(None, "row"), grid, cols,
        cols, cols, mids, P("row"), grid, cols, cols, cols,
    )
    return jax.shard_map(local, mesh=mesh, in_specs=in_specs, out_specs=out_specs, check_vma=False)
```

```python
from functools import partial

import jax
import jax.numpy as jnp
from jax import lax
from jax.experimental import pallas as pl
from jax.experimental.pallas import tpu as pltpu
from jax.sharding import PartitionSpec as P

HEAD = 64
LANES = 128
EPSILON = 1e-12
OFF = -1000000000.0
BF = jnp.bfloat16
F32 = jnp.float32
VMEM_LIMIT = 60 * 1024 * 1024


def nn(a, b):
    return lax.dot_general(a, b, (((1,), (0,)), ((), ())), preferred_element_type=F32)


def nt(a, b):
    return lax.dot_general(a, b, (((1,), (1,)), ((), ())), preferred_element_type=F32)


def tn(a, b):
    return lax.dot_general(a, b, (((0,), (0,)), ((), ())), preferred_element_type=F32)


def call(kernel, outs, spaces, scratch=(), out_spaces=None, flops=0, moved=0):
    memory = {"s": pltpu.SMEM, "v": pltpu.VMEM}
    return pl.pallas_call(
        kernel,
        out_shape=[jax.ShapeDtypeStruct(shape, dtype) for shape, dtype in outs],
        in_specs=[pl.BlockSpec(memory_space=memory[s]) for s in spaces],
        out_specs=[pl.BlockSpec(memory_space=memory[s]) for s in out_spaces or "v" * len(outs)],
        scratch_shapes=list(scratch),
        compiler_params=pltpu.CompilerParams(vmem_limit_bytes=VMEM_LIMIT),
        cost_estimate=pl.CostEstimate(flops=flops, bytes_accessed=moved, transcendentals=0),
    )


def rows_at(block, size):
    return pl.ds(pl.multiple_of(block * size, size), size)


def send_kernel(sizes, deal, where, x, *outs):
    groups, grid_rows, count, block = sizes
    pieces, table = outs[:groups], outs[groups]
    per_pair = count // groups
    g, r = where[0], where[1]
    mine = g * grid_rows + r
    for d in range(groups):
        base = (lax.rem(g + d, groups) * grid_rows + r) * count

        def step(j, rank):
            source = deal[base + j]
            table[d * per_pair + rank] = lax.rem(source, count)
            return rank + (lax.div(source, count) == mine).astype(jnp.int32)

        lax.fori_loop(0, count, step, jnp.int32(0), unroll=8)
        for rank in range(per_pair):
            rows = rows_at(table[d * per_pair + rank], block)
            pieces[d][rank * block : (rank + 1) * block, :] = x[rows, :]


def send_again_kernel(sizes, table, x, *outs):
    groups, grid_rows, count, block = sizes
    per_pair = count // groups
    for d in range(groups):
        for rank in range(per_pair):
            rows = rows_at(table[d * per_pair + rank], block)
            outs[d][rank * block : (rank + 1) * block, :] = x[rows, :]


def final_kernel(sizes, table, *refs):
    groups, grid_rows, count, block = sizes
    pieces, out = refs[:groups], refs[groups]
    per_pair = count // groups
    for d in range(groups):
        for rank in range(per_pair):
            rows = rows_at(table[(groups - d) % groups * per_pair + rank], block)
            out[rows, :] = pieces[d][rank * block : (rank + 1) * block, :]


def place_kernel(sizes, deal, where, table):
    groups, grid_rows, count, block = sizes
    per_pair = count // groups
    g, r = where[0], where[1]
    for k in range(grid_rows):
        base = (g * grid_rows + (r ^ k)) * count
        for d in range(groups):
            origin = lax.rem(g + groups - d, groups)

            def step(j, rank):
                table[k * count + d * per_pair + rank] = j
                return rank + (lax.div(deal[base + j], grid_rows * count) == origin).astype(jnp.int32)

            lax.fori_loop(0, count, step, jnp.int32(0), unroll=8)


def home_of(j, run, c):
    turn = lax.div(j, run)
    other = (lax.rem(turn, 2) != c).astype(jnp.int32)
    return other * 2 * run + lax.div(turn, 2) * run + lax.rem(j, run)


def arrive_kernel(sizes, run, place, where, *refs):
    groups, grid_rows, count, block = sizes
    pieces, own, other, both = refs[:groups], refs[groups], refs[groups + 1], refs[groups + 2]
    per_pair = count // groups
    for d in range(groups):
        for rank in range(per_pair):
            at = home_of(place[d * per_pair + rank], run, where[2])
            both[rows_at(at, block), :] = pieces[d][rank * block : (rank + 1) * block, :]
    own[...] = both[: own.shape[0], :]
    other[...] = both[own.shape[0] :, :]


def return_kernel(sizes, run, place, where, own, other, *refs):
    groups, grid_rows, count, block = sizes
    outs, both = refs[:groups], refs[groups]
    per_pair = count // groups
    both[: own.shape[0], :] = own[...]
    both[own.shape[0] :, :] = other[...]
    for d in range(groups):
        for rank in range(per_pair):
            at = home_of(place[(groups - d) % groups * per_pair + rank], run, where[2])
            outs[d][rank * block : (rank + 1) * block, :] = both[rows_at(at, block), :]


def sequence_ends(lengths, number):
    ends, total = [], jnp.int32(0)
    for s in range(number):
        total = total + lengths[0, s]
        ends.append(total)
    return ends


def sequence_of(ends, block):
    return sum((block >= end).astype(jnp.int32) for end in ends)


def first_of(ends, block):
    start = jnp.int32(0)
    for end in ends:
        start = jnp.where(block >= end, end, start)
    return start


def last_of(ends, block):
    stop = ends[-1]
    for end in reversed(ends):
        stop = jnp.where(block < end, end, stop)
    return stop


def thirds(v):
    one = v.astype(BF)
    rest = v - one.astype(F32)
    two = rest.astype(BF)
    three = (rest - two.astype(F32)).astype(BF)
    return one.astype(F32), two.astype(F32), three.astype(F32)


def attend_kernel(sizes, layout, heads, seqs, run, place, where, lengths, *refs):
    groups, grid_rows, count, block = sizes
    pieces = refs[: len(layout)]
    weights = refs[len(layout) : len(layout) + 2]
    bias = refs[len(layout) + 2]
    outs = refs[len(layout) + 3 :]
    q_ref, k_ref, v_ref, kt_ref, o_ref, xq_ref, own_ref = outs[:7]
    mixed = outs[7 : 7 + grid_rows]
    x_ref, score_ref, peak_ref, acc_ref = outs[7 + grid_rows :]
    r, c = where[1], where[2]
    ends = sequence_ends(lengths, seqs)
    half = weights[0].shape[1]
    inner = heads * HEAD
    rows = run * block
    for ref, (k, j, start) in zip(pieces, layout):
        for b in range(ref.shape[0] // block):
            at = (r ^ k) * count + place[k * count + start + b]
            x_ref[rows_at(at, block), j * half : (j + 1) * half] = ref[b * block : (b + 1) * block, :]
    local_runs = q_ref.shape[1] // rows
    shard_runs = local_runs // grid_rows
    lane = lax.broadcasted_iota(jnp.int32, (rows, HEAD), 1)
    down = lax.div(lax.broadcasted_iota(jnp.int32, (rows, HEAD), 0), block)
    ones_v = jnp.where(lane < 3, 1.0, 0.0)
    tail_k = (lane >= seqs) & (lane < seqs + 3)
    q_bias, v_bias = bias[0:1, :].astype(F32), bias[1:2, :].astype(F32)

    def project(i, mine):
        at = rows_at(i, rows)
        x0, x1 = x_ref[at, :half], x_ref[at, half:]
        first = 0 if mine else inner
        joined = nt(x0, weights[0][first:, :]) + nt(x1, weights[1][first:, :])
        flipped = nt(weights[0][inner : 2 * inner, :], x0) + nt(weights[1][inner : 2 * inner, :], x1)
        kt_ref[:, at] = flipped.astype(BF)
        seg = sequence_of(ends, down + i * run)
        key_tail = jnp.where((lane == seg) | tail_k, 1.0, 0.0)
        for h in range(heads):
            left = inner - first + h * HEAD
            value = joined[:, left + inner : left + inner + HEAD] + v_bias[:, h * HEAD : (h + 1) * HEAD]
            k_ref[h, at, :] = jnp.concatenate([joined[:, left : left + HEAD], key_tail], axis=1).astype(BF)
            v_ref[h, at, :] = jnp.concatenate([value, ones_v], axis=1).astype(BF)
        return at, joined, seg

    def pair(i, carry):
        project(2 * i + 1 - c, False)
        at, joined, seg = project(2 * i + c, True)
        here = rows_at(i, rows)
        query_tail = jnp.where((lane < seqs) & (lane != seg), OFF, 0.0)
        for h in range(heads):
            query = joined[:, h * HEAD : (h + 1) * HEAD] + q_bias[:, h * HEAD : (h + 1) * HEAD]
            query = query.astype(BF).astype(F32) * (HEAD**-0.5)
            q_ref[h, here, :] = jnp.concatenate([query, query_tail], axis=1).astype(BF)
        xq_ref[here, :] = x_ref[at, :]
        return carry

    lax.fori_loop(0, local_runs, pair, jnp.int32(0))
    own_ref[...] = xq_ref[rows_at(r, rows * shard_runs), :]
    wide = score_ref.shape[3]
    lane_q = lax.broadcasted_iota(jnp.int32, (rows, LANES), 1)

    def one_run(i, carry):
        first = i * 2 * run + c * run
        low = lax.div(first_of(ends, first) * block, wide)
        high = lax.div(last_of(ends, first + run - 1) * block + wide - 1, wide)
        here = rows_at(i, rows)
        peak_ref[...] = jnp.full_like(peak_ref, -3e38)

        def score(j, state):
            for h in range(heads):
                scores = nt(q_ref[h, here, :], k_ref[h, rows_at(j, wide), :])
                score_ref[h, j - low] = scores
                peak = peak_ref[h]
                for t in range(wide // LANES):
                    peak = jnp.maximum(peak, scores[:, t * LANES : (t + 1) * LANES])
                peak_ref[h] = peak
            return state

        lax.fori_loop(low, high, score, jnp.int32(0))
        tops = [jnp.max(peak_ref[h], axis=1, keepdims=True) for h in range(heads)]
        for h in range(heads):
            peak_ref[h] = jnp.broadcast_to(tops[h], (rows, LANES))
        acc_ref[...] = jnp.zeros_like(acc_ref)

        def mix(j, state):
            for h in range(heads):
                peak = jnp.concatenate([peak_ref[h]] * (wide // LANES), axis=1)
                part = jnp.exp(score_ref[h, j - low] - peak).astype(BF)
                acc_ref[h] += nn(part, v_ref[h, rows_at(j, wide), :])
            return state

        lax.fori_loop(low, high, mix, jnp.int32(0))
        for h in range(heads):
            acc = acc_ref[h]
            total = acc[:, HEAD : HEAD + 1]
            o_ref[h, here, :] = (acc[:, :HEAD] / total).astype(BF)
            kept = q_ref[h, here, :].astype(F32)
            for t, term in enumerate(thirds(tops[h] + jnp.log(total))):
                kept = jnp.where(lane_q == HEAD + seqs + t, -term, kept)
            q_ref[h, here, :] = kept.astype(BF)
        return carry

    lax.fori_loop(0, local_runs, one_run, jnp.int32(0))
    for k in range(grid_rows):
        cells = [
            o_ref[h, rows_at((r ^ k) * shard_runs + part, rows), :] for part in range(shard_runs) for h in range(heads)
        ]
        mixed[k][...] = jnp.concatenate(cells, axis=1)


def attend_back_kernel(grid_rows, heads, seqs, run, block, where, lengths, q_ref, k_ref, v_ref, kt_ref, o_ref, *refs):
    grads = refs[:grid_rows]
    dq_ref, own_ref, other_ref, do_ref, query_acc, key_acc, value_acc = refs[grid_rows:]
    r, c = where[1], where[2]
    ends = sequence_ends(lengths, seqs)
    rows = run * block
    wide = 2 * rows
    local_runs = q_ref.shape[1] // rows
    shard_runs = local_runs // grid_rows
    lane = lax.broadcasted_iota(jnp.int32, (rows, HEAD), 1)
    for k in range(grid_rows):
        for part in range(shard_runs):
            at = rows_at((r ^ k) * shard_runs + part, rows)
            for h in range(heads):
                left = (part * heads + h) * HEAD
                grad = grads[k][:, left : left + HEAD].astype(F32)
                centre = jnp.sum(grad * o_ref[h, at, :].astype(F32), axis=1, keepdims=True)
                tail = jnp.zeros((rows, HEAD), F32)
                for t, term in enumerate(thirds(centre)):
                    tail = jnp.where(lane == t, -term, tail)
                do_ref[h, at, :] = jnp.concatenate([grad, tail], axis=1).astype(BF)
    key_acc[...] = jnp.zeros_like(key_acc)
    value_acc[...] = jnp.zeros_like(value_acc)

    def one_run(i, carry):
        first = i * 2 * run + c * run
        low = lax.div(first_of(ends, first) * block, wide)
        high = lax.div(last_of(ends, first + run - 1) * block + wide - 1, wide)
        here = rows_at(i, rows)
        query_acc[...] = jnp.zeros_like(query_acc)

        def keys(j, state):
            at = rows_at(j, wide)
            for h in range(heads):
                query, grad = q_ref[h, here, :], do_ref[h, here, :]
                shares = jnp.exp(nt(k_ref[h, at, :], query))
                score_grads = (shares * nt(v_ref[h, at, :], grad)).astype(BF)
                value_acc[h, at, :] += nn(shares.astype(BF), grad)
                key_acc[h, at, :] += nn(score_grads, query)
                query_acc[h] += nn(kt_ref[h * HEAD : (h + 1) * HEAD, at], score_grads)
            return state

        lax.fori_loop(low, high, keys, jnp.int32(0))
        for h in range(heads):
            dq_ref[h, here, :] = (query_acc[h].T * (HEAD**-0.5)).astype(BF)
        return carry

    lax.fori_loop(0, local_runs, one_run, jnp.int32(0))

    def pair(i, carry):
        here = rows_at(i, rows)
        for h in range(heads):
            at = rows_at(2 * i + c, rows)
            own_ref[h, here, :] = jnp.concatenate([key_acc[h, at, :HEAD], value_acc[h, at, :HEAD]], axis=1)
            at = rows_at(2 * i + 1 - c, rows)
            other = jnp.concatenate([key_acc[h, at, :HEAD], value_acc[h, at, :HEAD]], axis=1)
            other_ref[h, here, :] = other.astype(BF)
        return carry

    lax.fori_loop(0, local_runs, pair, jnp.int32(0))


def join_kernel(grid_rows, heads, where, dq_ref, own_ref, got_ref, *refs):
    pieces, joined = refs[:grid_rows], refs[grid_rows]
    r = where[1]
    rows = pieces[0].shape[0]
    shard_runs = pieces[0].shape[1] // joined.shape[1]
    for k in range(grid_rows):
        cells = []
        for part in range(shard_runs):
            at = rows_at((r ^ k) * shard_runs + part, rows)
            both = [(own_ref[h, at, :] + got_ref[h, at, :].astype(F32)).astype(BF) for h in range(heads)]
            mine = [dq_ref[h, at, :] for h in range(heads)]
            mine += [b[:, :HEAD] for b in both] + [b[:, HEAD:] for b in both]
            joined[at, :] = jnp.concatenate(mine, axis=1)
            cells += mine
        pieces[k][...] = jnp.concatenate(cells, axis=1)


def project_in_grad_kernel(joined, xq, own, other):
    half = own.shape[1]
    wide = joined.shape[1]
    total = jnp.sum(joined[...].astype(F32), axis=0, keepdims=True)
    pad = jnp.zeros((1, 2 * half - wide), F32)
    total = jnp.concatenate([total, pad], axis=1)
    below = own.shape[0] - wide
    sums = jnp.concatenate([total[:, :half], total[:, half:], jnp.zeros((below - 2, half), F32)], axis=0).astype(BF)
    own[:wide, :] = tn(joined[...], xq[:, :half]).astype(BF)
    other[:wide, :] = tn(joined[...], xq[:, half:]).astype(BF)
    own[wide:, :] = sums
    other[wide:, :] = sums


def middle_kernel(plan, grid_rows, where, *refs):
    at = 0

    def take(n):
        nonlocal at
        got = refs[at : at + n]
        at += n
        return got

    mixed = take(grid_rows)
    (x_ref,) = take(1)
    dy = take(2)
    weights = take(2)
    outs = take(2)
    act_ref, up_grad_ref, hidden_ref, down_grad_ref, attn_grad_ref, grad_one_ref = take(6)
    mixed_grad = take(grid_rows)
    (small,) = take(1)
    (slope_ref,) = take(1)
    half = dy[0].shape[1]
    width = 2 * half
    inner = mixed[0].shape[1] // 2
    rows = mixed[0].shape[0]
    r, c = where[1], where[2]
    small[...] = jnp.zeros_like(small)
    first = [weights[0].at[(r ^ k) * 2 + (c ^ j)] for k in range(grid_rows) for j in range(2)]
    second = [weights[1].at[(r ^ k) * 2 + (c ^ j)] for k in range(grid_rows) for j in range(2)]

    def vector(index):
        row = plan["vectors"] + index
        return jnp.concatenate([second[0][row : row + 1, :], second[1][row : row + 1, :]], axis=1).astype(F32)

    output_bias, first_gain, first_shift, down_bias, second_gain, second_shift = (vector(i) for i in range(6))

    def mean(v):
        return jnp.sum(v, axis=1, keepdims=True) / width

    def norm(v):
        centred = v - mean(v)
        inverse = lax.rsqrt(mean(centred * centred) + EPSILON)
        return centred * inverse, inverse

    def norm_back(v, normed, inverse):
        return inverse * (v - mean(v) - normed * mean(v * normed))

    def total(v):
        return jnp.sum(v, axis=0, keepdims=True)

    def keep(row, v):
        small[row : row + 1, :] += v

    for part in range(2):
        span = slice(part * rows, (part + 1) * rows)
        lanes = slice(part * inner, (part + 1) * inner)
        parts = []
        for j in range(2):
            parts.append(sum(nn(mixed[k][:, lanes], first[2 * k + j][plan["out"], :]) for k in range(grid_rows)))
        attention = jnp.concatenate(parts, axis=1) + output_bias
        normed_one, inverse_one = norm(x_ref[span, :].astype(F32) + attention)
        hidden = normed_one * first_gain + first_shift
        low = hidden.astype(BF)
        hidden_ref[span, :] = low
        downs = [jnp.zeros((rows, half), F32), jnp.zeros((rows, half), F32)]
        for k in range(grid_rows):
            for u in range(2):
                cols = slice((2 * k + u) * half, (2 * k + u + 1) * half)
                up_rows = plan["up"][u]
                upward = nn(low[:, :half], first[2 * k][up_rows, :]) + nn(low[:, half:], first[2 * k + 1][up_rows, :])
                upward = upward + first[2 * k][plan["up_bias"] + u : plan["up_bias"] + u + 1, :].astype(F32)
                bell = (1.0 + lax.erf(upward * (2.0**-0.5))) * 0.5
                slope_ref[:, cols] = bell + upward * jnp.exp(upward * upward * -0.5) * 0.3989422804014327
                act = (upward * bell).astype(BF)
                act_ref[span, cols] = act
                down_rows = plan["down"][u]
                for j in range(2):
                    downs[j] = downs[j] + nn(act, second[2 * k + j][down_rows, :])
        downward = jnp.concatenate(downs, axis=1) + down_bias
        normed_two, inverse_two = norm(hidden + downward)
        final = (normed_two * second_gain + second_shift).astype(BF)
        outs[0][span, :] = final[:, :half]
        outs[1][span, :] = final[:, half:]
        grad_out = jnp.concatenate([dy[0][span, :], dy[1][span, :]], axis=1).astype(F32)
        keep(0, total(grad_out * normed_two))
        keep(1, total(grad_out))
        grad_two = norm_back(grad_out * second_gain, normed_two, inverse_two)
        down_grad = grad_two.astype(BF)
        down_grad_ref[span, :] = down_grad
        keep(4, total(down_grad.astype(F32)))
        grads = [grad_two[:, :half], grad_two[:, half:]]
        for k in range(grid_rows):
            for u in range(2):
                cols = slice((2 * k + u) * half, (2 * k + u + 1) * half)
                up_rows, down_rows = plan["up"][u], plan["down"][u]
                act_grad = nt(down_grad[:, :half], second[2 * k][down_rows, :]) + nt(
                    down_grad[:, half:], second[2 * k + 1][down_rows, :]
                )
                up_grad = (act_grad * slope_ref[:, cols]).astype(BF)
                up_grad_ref[span, cols] = up_grad
                small[8 + k : 9 + k, u * half : (u + 1) * half] += total(up_grad.astype(F32))
                for j in range(2):
                    grads[j] = grads[j] + nt(up_grad, first[2 * k + j][up_rows, :])
        grad_hidden = jnp.concatenate(grads, axis=1)
        keep(2, total(grad_hidden * normed_one))
        keep(3, total(grad_hidden))
        grad_one = norm_back(grad_hidden * first_gain, normed_one, inverse_one)
        grad_one_ref[span, :] = grad_one
        attn_grad = grad_one.astype(BF)
        attn_grad_ref[span, :] = attn_grad
        keep(5, total(attn_grad.astype(F32)))
        for k in range(grid_rows):
            back = nt(attn_grad[:, :half], first[2 * k][plan["out"], :]) + nt(
                attn_grad[:, half:], first[2 * k + 1][plan["out"], :]
            )
            mixed_grad[k][:, lanes] = back.astype(BF)


def middle_grad_kernel(plan, grid_rows, *refs):
    mixed = refs[:grid_rows]
    act, up_grad, hidden, down_grad, attn_grad, small = refs[grid_rows : grid_rows + 6]
    first, second = refs[grid_rows + 6 : grid_rows + 8], refs[grid_rows + 8 : grid_rows + 10]
    half = hidden.shape[1] // 2
    rows, inner = mixed[0].shape[0], mixed[0].shape[1] // 2
    for j in range(2):
        side = slice(j * half, (j + 1) * half)
        for place, k in enumerate(plan["second_order"]):
            for u in range(2):
                cols = slice((2 * k + u) * half, (2 * k + u + 1) * half)
                second[j][place, plan["down"][u], :] = tn(act[:, cols], down_grad[:, side]).astype(BF)
            sums = [small[:6, side], small[8 + k : 9 + k, :half], small[8 + k : 9 + k, half:]]
            sums += [jnp.zeros((second[j].shape[1] - plan["sums"] - 8, half), F32)]
            second[j][place, plan["sums"] :, :] = jnp.concatenate(sums, axis=0).astype(BF)
        for place, k in enumerate(plan["first_order"]):
            for u in range(2):
                cols = slice((2 * k + u) * half, (2 * k + u + 1) * half)
                first[j][place, plan["up"][u], :] = tn(hidden[:, side], up_grad[:, cols]).astype(BF)
            back = tn(mixed[k][:, :inner], attn_grad[:rows, side]) + tn(mixed[k][:, inner:], attn_grad[rows:, side])
            first[j][place, plan["out"], :] = back.astype(BF)


def input_grad_kernel(grid_rows, where, *refs):
    pieces = refs[:grid_rows]
    weight, grad_one, own, other = refs[grid_rows:]
    r, c = where[1], where[2]
    half = own.shape[1]
    rows = pieces[0].shape[0]
    wide = weight.shape[1]
    for part in range(2):
        span = slice(part * rows, (part + 1) * rows)
        for j, out in enumerate((own, other)):
            total = grad_one[span, j * half : (j + 1) * half]
            for k in range(grid_rows):
                total = total + nn(pieces[k][:, part * wide : (part + 1) * wide], weight[(r ^ k) * 2 + (c ^ j)])
            out[span, :] = total.astype(BF)


def shift(array, axis, to):
    return lax.ppermute(array, axis, [(i, to(i)) for i in range(lax.axis_size(axis))])


def to_row(array, k):
    return shift(array, "row", lambda i: i ^ k)


def to_col(array):
    return shift(array, "col", lambda i: 1 - i)


def after(array, *earlier):
    return lax.optimization_barrier((array, *earlier))[0]


def gather_row(array, block):
    near, side = to_row(array, 1), to_row(array, 2)
    cut = array.shape[0] // (2 * block) * block
    got = [(0, 0, array), (1, 0, near), (2, 0, side)]
    if cut:
        got += [(3, 0, to_row(near[:cut], 2))]
    return got + [(3, cut, to_row(side[cut:], 1))]


def add(*arrays):
    return sum(a.astype(F32) for a in arrays).astype(BF)


def reduce_row(own, got, turn):
    first, then = (1, 2) if turn == 0 else (2, 1)
    came = to_row(add(own[2:], got[2:]), first)
    last = to_row(add(own[1], got[1], came[1]), then)
    return add(own[0], got[0], came[0], last)


def reduce_groups(array, group):
    if lax.axis_size("tok") != 4:
        return lax.psum(array, "tok")
    side = (group ^ (group >> 1)) & 1
    middle = array.shape[0] // 2
    low, high = array[:middle], array[middle:]
    half = add(jnp.where(side == 0, low, high), shift(jnp.where(side == 0, high, low), "tok", lambda i: i ^ 1))
    half = add(half, shift(half, "tok", lambda i: i ^ 3))
    rest = shift(half, "tok", lambda i: i ^ 1)
    return jnp.concatenate([jnp.where(side == 0, half, rest), jnp.where(side == 0, rest, half)], axis=0)


def local(
    tokens,
    cotangent,
    lengths,
    dealing,
    project_in,
    project_bias,
    project_out,
    output_bias,
    first_gain,
    first_shift,
    up_weight,
    up_bias,
    down_weight,
    down_bias,
    second_gain,
    second_shift,
):
    groups, grid_rows = lax.axis_size("tok"), lax.axis_size("row")
    group, row, col = lax.axis_index("tok"), lax.axis_index("row"), lax.axis_index("col")
    where = jnp.stack([group, row, col]).astype(jnp.int32)
    shard_rows, half = tokens.shape
    width = 2 * half
    count = dealing.shape[0] // (groups * grid_rows)
    block = shard_rows // count
    sizes = (groups, grid_rows, count, block)
    seqs = lengths.shape[1]
    inner = project_bias.shape[1]
    heads = inner // HEAD
    hidden_part = up_weight.shape[1]
    run = count // 4
    rows = run * block
    own_rows = shard_rows // 2
    half_rows = own_rows * grid_rows
    wide = 3 * inner
    per_pair = count // groups
    piece = (per_pair * block, half)
    shard = (shard_rows, half)
    both = pltpu.VMEM(shard, BF)

    def exchange(pieces):
        return [shift(p, "tok", lambda i, d=d: (i + d) % groups) if d else p for d, p in enumerate(pieces)]

    vectors = jnp.stack([output_bias, first_gain, first_shift, down_bias, second_gain, second_shift])
    up_bias_rows = up_bias.reshape(2, half)
    first_weights = jnp.concatenate(
        [up_weight[:, :half], up_weight[:, half:], project_out, jnp.pad(up_bias_rows, ((0, 14), (0, 0)))], axis=0
    )
    second_weights = jnp.concatenate([down_weight, jnp.pad(vectors, ((0, 10), (0, 0)))], axis=0)
    joined_weight = project_in.transpose(1, 2, 0).reshape(wide, half)
    plan = {
        "up": (slice(0, half), slice(half, 2 * half)),
        "out": slice(2 * half, 2 * half + inner),
        "up_bias": 2 * half + inner,
        "down": (slice(0, half), slice(half, 2 * half)),
        "vectors": hidden_part,
        "sums": hidden_part,
        "first_order": (0, 2, 1, 3),
        "second_order": (0, 1, 2, 3),
    }

    *sent, table = call(
        partial(send_kernel, sizes), [(piece, BF)] * groups + [((count + 8,), jnp.int32)], "ssv",
        out_spaces="v" * groups + "s",
    )(dealing, where, tokens)
    (place,) = call(partial(place_kernel, sizes), [((grid_rows * count + 8,), jnp.int32)], "ss", out_spaces="s")(
        dealing, where
    )
    got = exchange(sent)
    layout, pieces = [], []
    for start, chunk in ((0, got[0]), (per_pair, jnp.concatenate(got[1:], axis=0))):
        for k, top, part in gather_row(chunk, block):
            layout += [(k, 0, start + top // block), (k, 1, start + top // block)]
            pieces += [part, to_col(part)]
    first_all = lax.all_gather(first_weights, ("row", "col"))
    second_all = lax.all_gather(second_weights, ("row", "col"))
    wide_keys = 2 * rows
    q, k, v, kt, mixed_own, xq, x_own, *mixed = call(
        partial(attend_kernel, sizes, layout, heads, seqs, run),
        [
            ((heads, half_rows, LANES), BF),
            ((heads, 2 * half_rows, LANES), BF),
            ((heads, 2 * half_rows, LANES), BF),
            ((inner, 2 * half_rows), BF),
            ((heads, half_rows, HEAD), BF),
            ((half_rows, width), BF),
            ((own_rows, width), BF),
        ]
        + [((rows, 2 * inner), BF)] * grid_rows,
        "sss" + "v" * (len(pieces) + 3),
        [
            pltpu.VMEM((2 * half_rows, width), BF),
            pltpu.VMEM((heads, 2 * half_rows // wide_keys, rows, wide_keys), F32),
            pltpu.VMEM((heads, rows, LANES), F32),
            pltpu.VMEM((heads, rows, LANES), F32),
        ],
    )(place, where, lengths, *pieces, joined_weight, to_col(joined_weight), project_bias)

    dy_sent = call(partial(send_again_kernel, sizes), [(piece, BF)] * groups, "sv")(table, after(cotangent, *got))
    dy_own, dy_other = call(
        partial(arrive_kernel, sizes, run), [((own_rows, half), BF)] * 2, "ss" + "v" * groups, [both]
    )(place, where, *exchange(dy_sent))
    dy = [dy_own, to_col(dy_other)]

    def send_back(own, other):
        pieces = call(partial(return_kernel, sizes, run), [(piece, BF)] * groups, "ssvv", [both])(place, where, own, other)
        return call(partial(final_kernel, sizes), [(shard, BF)], "s" + "v" * groups)(table, *exchange(pieces))[0]

    mixed_got = [to_row(m, i) if i else m for i, m in enumerate(mixed)]
    joined_all = lax.all_gather(after(joined_weight, *mixed_got), ("row", "col"))
    hidden_all = grid_rows * hidden_part
    out0, out1, act, up_grad, hidden, down_grad, attn_grad, grad_one, *rest = call(
        partial(middle_kernel, plan, grid_rows),
        [
            ((own_rows, half), BF),
            ((own_rows, half), BF),
            ((own_rows, hidden_all), BF),
            ((own_rows, hidden_all), BF),
            ((own_rows, width), BF),
            ((own_rows, width), BF),
            ((own_rows, width), BF),
            ((own_rows, width), F32),
        ]
        + [((rows, 2 * inner), BF)] * grid_rows
        + [((8 + 8, width), F32)],
        "s" + "v" * (grid_rows + 3 + 2),
        [pltpu.VMEM((rows, hidden_all), F32)],
    )(where, *mixed_got, x_own, *dy, first_all, second_all)
    mixed_grad, small = rest[:grid_rows], rest[grid_rows]
    mixed_grad_got = [to_row(m, i) if i else m for i, m in enumerate(mixed_grad)]

    first_rows, second_rows = 2 * half + inner, hidden_part + 32
    first_own, first_other, second_own, second_other = call(
        partial(middle_grad_kernel, plan, grid_rows),
        [((grid_rows, first_rows, half), BF)] * 2 + [((grid_rows, second_rows, half), BF)] * 2,
        "v" * (grid_rows + 6),
    )(*mixed_got, act, up_grad, hidden, down_grad, attn_grad, small)
    first_sum = reduce_groups(reduce_row(first_own, to_col(first_other), 0), group)
    second_sum = reduce_groups(reduce_row(second_own, to_col(second_other), 1), group)

    output = send_back(out0, to_col(out1))

    dq, kv_own, kv_other = call(
        partial(attend_back_kernel, grid_rows, heads, seqs, run, block),
        [
            ((heads, half_rows, HEAD), BF),
            ((heads, half_rows, LANES), F32),
            ((heads, half_rows, LANES), BF),
        ],
        "ss" + "v" * (5 + grid_rows),
        [
            pltpu.VMEM((heads, half_rows, LANES), BF),
            pltpu.VMEM((heads, HEAD, rows), F32),
            pltpu.VMEM((heads, 2 * half_rows, LANES), F32),
            pltpu.VMEM((heads, 2 * half_rows, LANES), F32),
        ],
    )(where, lengths, q, k, v, kt, mixed_own, *mixed_grad_got)
    *joined_pieces, joined = call(
        partial(join_kernel, grid_rows, heads),
        [((rows, 2 * wide), BF)] * grid_rows + [((half_rows, wide), BF)],
        "svvv",
    )(where, dq, kv_own, to_col(kv_other))
    joined_got = [to_row(m, i) if i else m for i, m in enumerate(joined_pieces)]
    in_own, in_other = call(project_in_grad_kernel, [((wide + 32, half), BF)] * 2, "vv")(joined, xq)
    in_sum = reduce_groups(add(in_own, to_col(in_other)), group)
    dx_own, dx_other = call(
        partial(input_grad_kernel, grid_rows), [((own_rows, half), BF)] * 2, "s" + "v" * (grid_rows + 2)
    )(where, *joined_got, joined_all, grad_one)
    input_grad = send_back(dx_own, to_col(dx_other))

    project_in_grad = in_sum[:wide].reshape(3, inner, half).transpose(2, 0, 1)
    sums = in_sum[wide : wide + 2].reshape(2 * half)
    sums = [sums[:inner], sums[2 * inner : 3 * inner]]
    tail = second_sum[hidden_part : hidden_part + 8].astype(F32)
    return (
        output,
        input_grad,
        project_in_grad.astype(F32),
        jnp.stack(sums).astype(F32),
        first_sum[2 * half :].astype(F32),
        tail[5],
        tail[2],
        tail[3],
        jnp.concatenate([first_sum[:half], first_sum[half : 2 * half]], axis=1).astype(F32),
        tail[6:8].reshape(hidden_part),
        second_sum[:hidden_part].astype(F32),
        tail[4],
        tail[0],
        tail[1],
    )


def solution(mesh):
    stream, grid = P(("tok", "row"), "col"), P("row", "col")
    joined, mids, cols = P("col", None, "row"), P("col", "row"), P("col")
    in_specs = (
        stream, stream, P("tok", None), P(), joined, P(None, "row"), grid, cols,
        cols, cols, mids, P("row"), grid, cols, cols, cols,
    )
    out_specs = (
        stream, stream, joined, P(None, "row"), grid, cols,
        cols, cols, mids, P("row"), grid, cols, cols, cols,
    )
    return jax.shard_map(local, mesh=mesh, in_specs=in_specs, out_specs=out_specs, check_vma=False)
```

```python
from functools import partial

import jax
import jax.numpy as jnp
from jax import lax
from jax.experimental import pallas as pl
from jax.experimental.pallas import tpu as pltpu
from jax.sharding import PartitionSpec as P

HEAD = 64
LANES = 128
EPSILON = 1e-12
OFF = -1000000000.0
BF = jnp.bfloat16
F32 = jnp.float32
VMEM_LIMIT = 60 * 1024 * 1024


def nn(a, b):
    return lax.dot_general(a, b, (((1,), (0,)), ((), ())), preferred_element_type=F32)


def nt(a, b):
    return lax.dot_general(a, b, (((1,), (1,)), ((), ())), preferred_element_type=F32)


def tn(a, b):
    return lax.dot_general(a, b, (((0,), (0,)), ((), ())), preferred_element_type=F32)


def call(kernel, outs, spaces, scratch=(), out_spaces=None, us=2, blocks=()):
    memory = {"s": pltpu.SMEM, "v": pltpu.VMEM}
    specs = [pl.BlockSpec(memory_space=memory[s]) for s in spaces]
    for operand, (shape, index) in dict(blocks).items():
        specs[operand] = pl.BlockSpec(
            shape, lambda i, index=index, rank=len(shape): (index,) + (0,) * (rank - 1), pipeline_mode=pl.Buffered(1)
        )
    return pl.pallas_call(
        kernel,
        out_shape=[jax.ShapeDtypeStruct(shape, dtype) for shape, dtype in outs],
        grid=(1,) if blocks else (),
        in_specs=specs,
        out_specs=[pl.BlockSpec(memory_space=memory[s]) for s in out_spaces or "v" * len(outs)],
        scratch_shapes=list(scratch),
        compiler_params=pltpu.CompilerParams(vmem_limit_bytes=VMEM_LIMIT),
        cost_estimate=pl.CostEstimate(flops=us * 3 * 10**8, bytes_accessed=us * 10**6, transcendentals=0),
    )


def rows_at(block, size):
    return pl.ds(pl.multiple_of(block * size, size), size)


def send_kernel(sizes, deal, where, x, *outs):
    groups, grid_rows, count, block = sizes
    pieces, table = outs[:groups], outs[groups]
    per_pair = count // groups
    g, r = where[0], where[1]
    mine = g * grid_rows + r
    for d in range(groups):
        base = (lax.rem(g + d, groups) * grid_rows + r) * count

        def step(j, rank):
            source = deal[base + j]
            table[d * per_pair + rank] = lax.rem(source, count)
            return rank + (lax.div(source, count) == mine).astype(jnp.int32)

        lax.fori_loop(0, count, step, jnp.int32(0), unroll=8)
        for rank in range(per_pair):
            rows = rows_at(table[d * per_pair + rank], block)
            pieces[d][rank * block : (rank + 1) * block, :] = x[rows, :]


def send_again_kernel(sizes, table, x, *outs):
    groups, grid_rows, count, block = sizes
    per_pair = count // groups
    for d in range(groups):
        for rank in range(per_pair):
            rows = rows_at(table[d * per_pair + rank], block)
            outs[d][rank * block : (rank + 1) * block, :] = x[rows, :]


def final_kernel(sizes, table, *refs):
    groups, grid_rows, count, block = sizes
    pieces, out = refs[:groups], refs[groups]
    per_pair = count // groups
    for d in range(groups):
        for rank in range(per_pair):
            rows = rows_at(table[(groups - d) % groups * per_pair + rank], block)
            out[rows, :] = pieces[d][rank * block : (rank + 1) * block, :]


def place_kernel(sizes, deal, where, table, tally):
    groups, grid_rows, count, block = sizes
    per_pair = count // groups
    g, r = where[0], where[1]
    for k in range(grid_rows):
        base = (g * grid_rows + (r ^ k)) * count
        for d in range(groups):
            tally[d] = k * count + d * per_pair

        def step(j, carry):
            d = lax.rem(g - lax.div(deal[base + j], grid_rows * count) + groups, groups)
            at = tally[d]
            table[at] = j
            tally[d] = at + 1
            return carry

        lax.fori_loop(0, count, step, jnp.int32(0), unroll=8)


def home_of(j, run, c):
    turn = lax.div(j, run)
    other = (lax.rem(turn, 2) != c).astype(jnp.int32)
    return other * 2 * run + lax.div(turn, 2) * run + lax.rem(j, run)


def arrive_kernel(sizes, run, place, where, *refs):
    groups, grid_rows, count, block = sizes
    pieces, own, other, both = refs[:groups], refs[groups], refs[groups + 1], refs[groups + 2]
    per_pair = count // groups
    for d in range(groups):
        for rank in range(per_pair):
            at = home_of(place[d * per_pair + rank], run, where[2])
            both[rows_at(at, block), :] = pieces[d][rank * block : (rank + 1) * block, :]
    own[...] = both[: own.shape[0], :]
    other[...] = both[own.shape[0] :, :]


def return_kernel(sizes, run, place, where, own, other, *refs):
    groups, grid_rows, count, block = sizes
    outs, both = refs[:groups], refs[groups]
    per_pair = count // groups
    rows = own.shape[0]
    both[:rows, :] = own[...]
    both[rows:, :] = other[other.shape[0] - rows :, :]
    for d in range(groups):
        for rank in range(per_pair):
            at = home_of(place[(groups - d) % groups * per_pair + rank], run, where[2])
            outs[d][rank * block : (rank + 1) * block, :] = both[rows_at(at, block), :]


def sequence_ends(lengths, number):
    ends, total = [], jnp.int32(0)
    for s in range(number):
        total = total + lengths[0, s]
        ends.append(total)
    return ends


def sequence_of(ends, block):
    return sum((block >= end).astype(jnp.int32) for end in ends)


def first_of(ends, block):
    start = jnp.int32(0)
    for end in ends:
        start = jnp.where(block >= end, end, start)
    return start


def last_of(ends, block):
    stop = ends[-1]
    for end in reversed(ends):
        stop = jnp.where(block < end, end, stop)
    return stop


def thirds(v):
    one = v.astype(BF)
    rest = v - one.astype(F32)
    two = rest.astype(BF)
    three = (rest - two.astype(F32)).astype(BF)
    return one.astype(F32), two.astype(F32), three.astype(F32)


def attend_kernel(sizes, layout, heads, seqs, run, place, where, lengths, *refs):
    groups, grid_rows, count, block = sizes
    pieces = refs[: len(layout)]
    weights = refs[len(layout) : len(layout) + 2]
    bias = refs[len(layout) + 2]
    outs = refs[len(layout) + 3 :]
    q_ref, k_ref, v_ref, kt_ref, o_ref, xq_ref, own_ref = outs[:7]
    mixed = outs[7 : 7 + grid_rows]
    x_ref, score_ref, peak_ref, acc_ref = outs[7 + grid_rows :]
    r, c = where[1], where[2]
    ends = sequence_ends(lengths, seqs)
    half = weights[0].shape[1]
    inner = heads * HEAD
    rows = run * block
    for ref, (k, j, start) in zip(pieces, layout):
        for b in range(ref.shape[0] // block):
            at = (r ^ k) * count + place[k * count + start + b]
            x_ref[rows_at(at, block), j * half : (j + 1) * half] = ref[b * block : (b + 1) * block, :]
    local_runs = q_ref.shape[1] // rows
    shard_runs = local_runs // grid_rows
    lane = lax.broadcasted_iota(jnp.int32, (rows, HEAD), 1)
    down = lax.div(lax.broadcasted_iota(jnp.int32, (rows, HEAD), 0), block)
    ones_v = jnp.where(lane < 3, 1.0, 0.0)
    tail_k = (lane >= seqs) & (lane < seqs + 3)
    q_bias, v_bias = bias[0:1, :].astype(F32), bias[1:2, :].astype(F32)

    def project(i, mine):
        at = rows_at(i, rows)
        x0, x1 = x_ref[at, :half], x_ref[at, half:]
        first = 0 if mine else inner
        joined = nt(x0, weights[0][first:, :]) + nt(x1, weights[1][first:, :])
        flipped = nt(weights[0][inner : 2 * inner, :], x0) + nt(weights[1][inner : 2 * inner, :], x1)
        kt_ref[:, at] = flipped.astype(BF)
        seg = sequence_of(ends, down + i * run)
        key_tail = jnp.where((lane == seg) | tail_k, 1.0, 0.0)
        for h in range(heads):
            left = inner - first + h * HEAD
            value = joined[:, left + inner : left + inner + HEAD] + v_bias[:, h * HEAD : (h + 1) * HEAD]
            k_ref[h, at, :] = jnp.concatenate([joined[:, left : left + HEAD], key_tail], axis=1).astype(BF)
            v_ref[h, at, :] = jnp.concatenate([value, ones_v], axis=1).astype(BF)
        return at, joined, seg

    def pair(i, carry):
        project(2 * i + 1 - c, False)
        at, joined, seg = project(2 * i + c, True)
        here = rows_at(i, rows)
        query_tail = jnp.where((lane < seqs) & (lane != seg), OFF, 0.0)
        for h in range(heads):
            query = joined[:, h * HEAD : (h + 1) * HEAD] + q_bias[:, h * HEAD : (h + 1) * HEAD]
            query = query.astype(BF).astype(F32) * (HEAD**-0.5)
            q_ref[h, here, :] = jnp.concatenate([query, query_tail], axis=1).astype(BF)
        xq_ref[here, :] = x_ref[at, :]
        return carry

    lax.fori_loop(0, local_runs, pair, jnp.int32(0))
    own_ref[...] = xq_ref[rows_at(r, rows * shard_runs), :]
    wide = score_ref.shape[3]
    lane_q = lax.broadcasted_iota(jnp.int32, (rows, LANES), 1)

    def one_run(i, carry):
        first = i * 2 * run + c * run
        low = lax.div(first_of(ends, first) * block, wide)
        high = lax.div(last_of(ends, first + run - 1) * block + wide - 1, wide)
        here = rows_at(i, rows)
        peak_ref[...] = jnp.full_like(peak_ref, -3e38)

        def score(j, state):
            for h in range(heads):
                scores = nt(q_ref[h, here, :], k_ref[h, rows_at(j, wide), :])
                score_ref[h, j - low] = scores
                peak = peak_ref[h]
                for t in range(wide // LANES):
                    peak = jnp.maximum(peak, scores[:, t * LANES : (t + 1) * LANES])
                peak_ref[h] = peak
            return state

        lax.fori_loop(low, high, score, jnp.int32(0))
        tops = [jnp.max(peak_ref[h], axis=1, keepdims=True) for h in range(heads)]
        for h in range(heads):
            peak_ref[h] = jnp.broadcast_to(tops[h], (rows, LANES))
        acc_ref[...] = jnp.zeros_like(acc_ref)

        def mix(j, state):
            for h in range(heads):
                peak = jnp.concatenate([peak_ref[h]] * (wide // LANES), axis=1)
                part = jnp.exp(score_ref[h, j - low] - peak).astype(BF)
                acc_ref[h] += nn(part, v_ref[h, rows_at(j, wide), :])
            return state

        lax.fori_loop(low, high, mix, jnp.int32(0))
        for h in range(heads):
            acc = acc_ref[h]
            total = acc[:, HEAD : HEAD + 1]
            o_ref[h, here, :] = (acc[:, :HEAD] / total).astype(BF)
            kept = q_ref[h, here, :].astype(F32)
            for t, term in enumerate(thirds(tops[h] + jnp.log(total))):
                kept = jnp.where(lane_q == HEAD + seqs + t, -term, kept)
            q_ref[h, here, :] = kept.astype(BF)
        return carry

    lax.fori_loop(0, local_runs, one_run, jnp.int32(0))
    for k in range(grid_rows):
        cells = [
            o_ref[h, rows_at((r ^ k) * shard_runs + part, rows), :] for part in range(shard_runs) for h in range(heads)
        ]
        mixed[k][...] = jnp.concatenate(cells, axis=1)


def attend_back_kernel(
    grid_rows, heads_all, start, seqs, run, block, where, lengths, q_ref, k_ref, v_ref, kt_ref, o_ref, *refs
):
    grads = refs[:grid_rows]
    dq_ref, own_ref, other_ref, do_ref, query_acc, key_acc, value_acc = refs[grid_rows:]
    r, c = where[1], where[2]
    heads = q_ref.shape[0]
    ends = sequence_ends(lengths, seqs)
    rows = run * block
    wide = 2 * rows
    local_runs = q_ref.shape[1] // rows
    shard_runs = local_runs // grid_rows
    lane = lax.broadcasted_iota(jnp.int32, (rows, HEAD), 1)
    for k in range(grid_rows):
        for part in range(shard_runs):
            at = rows_at((r ^ k) * shard_runs + part, rows)
            for h in range(heads):
                left = (part * heads_all + start + h) * HEAD
                grad = grads[k][:, left : left + HEAD].astype(F32)
                centre = jnp.sum(grad * o_ref[h, at, :].astype(F32), axis=1, keepdims=True)
                tail = jnp.zeros((rows, HEAD), F32)
                for t, term in enumerate(thirds(centre)):
                    tail = jnp.where(lane == t, -term, tail)
                do_ref[h, at, :] = jnp.concatenate([grad, tail], axis=1).astype(BF)
    key_acc[...] = jnp.zeros_like(key_acc)
    value_acc[...] = jnp.zeros_like(value_acc)

    def one_run(i, carry):
        first = i * 2 * run + c * run
        low = lax.div(first_of(ends, first) * block, wide)
        high = lax.div(last_of(ends, first + run - 1) * block + wide - 1, wide)
        here = rows_at(i, rows)
        query_acc[...] = jnp.zeros_like(query_acc)

        def keys(j, state):
            at = rows_at(j, wide)
            for h in range(heads):
                query, grad = q_ref[h, here, :], do_ref[h, here, :]
                shares = jnp.exp(nt(k_ref[h, at, :], query))
                score_grads = (shares * nt(v_ref[h, at, :], grad)).astype(BF)
                value_acc[h, at, :] += nn(shares.astype(BF), grad)
                key_acc[h, at, :] += nn(score_grads, query)
                query_acc[h] += nn(kt_ref[h * HEAD : (h + 1) * HEAD, at], score_grads)
            return state

        lax.fori_loop(low, high, keys, jnp.int32(0))
        for h in range(heads):
            dq_ref[h, here, :] = (query_acc[h].T * (HEAD**-0.5)).astype(BF)
        return carry

    lax.fori_loop(0, local_runs, one_run, jnp.int32(0))

    def pair(i, carry):
        here = rows_at(i, rows)
        for h in range(heads):
            at = rows_at(2 * i + c, rows)
            own_ref[h, here, :] = jnp.concatenate([key_acc[h, at, :HEAD], value_acc[h, at, :HEAD]], axis=1)
            at = rows_at(2 * i + 1 - c, rows)
            other = jnp.concatenate([key_acc[h, at, :HEAD], value_acc[h, at, :HEAD]], axis=1)
            other_ref[h, here, :] = other.astype(BF)
        return carry

    lax.fori_loop(0, local_runs, pair, jnp.int32(0))


def join_kernel(grid_rows, where, dq_ref, own_ref, got_ref, *refs):
    pieces, joined = refs[:grid_rows], refs[grid_rows]
    r = where[1]
    heads, rows = dq_ref.shape[0], pieces[0].shape[0]
    shard_runs = pieces[0].shape[1] // joined.shape[1]
    for k in range(grid_rows):
        cells = []
        for part in range(shard_runs):
            at = rows_at((r ^ k) * shard_runs + part, rows)
            both = [(own_ref[h, at, :] + got_ref[h, at, :].astype(F32)).astype(BF) for h in range(heads)]
            mine = [dq_ref[h, at, :] for h in range(heads)]
            mine += [b[:, :HEAD] for b in both] + [b[:, HEAD:] for b in both]
            joined[at, :] = jnp.concatenate(mine, axis=1)
            cells += mine
        pieces[k][...] = jnp.concatenate(cells, axis=1)


def project_in_grad_kernel(*refs):
    joined, (xq, own, other) = refs[:-3], refs[-3:]
    half = own.shape[1]
    top, totals = 0, []
    for part in joined:
        wide = part.shape[1]
        own[top : top + wide, :] = tn(part[...], xq[:, :half]).astype(BF)
        other[top : top + wide, :] = tn(part[...], xq[:, half:]).astype(BF)
        totals.append(jnp.sum(part[...].astype(F32), axis=0, keepdims=True))
        top += wide
    total = jnp.concatenate([*totals, jnp.zeros((1, 2 * half - top), F32)], axis=1)
    below = own.shape[0] - top
    sums = jnp.concatenate([total[:, :half], total[:, half:], jnp.zeros((below - 2, half), F32)], axis=0).astype(BF)
    own[top:, :] = sums
    other[top:, :] = sums


def middle_kernel(plan, grid_rows, where, *refs):
    at = 0

    def take(n):
        nonlocal at
        got = refs[at : at + n]
        at += n
        return got

    r, c = where[1], where[2]
    mixed = take(grid_rows)
    (x_ref,) = take(1)
    dy = take(2)
    first = take(2 * grid_rows)
    (gathered,) = take(1)
    second = [gathered.at[(r ^ k) * 2 + (c ^ j)] for k in range(grid_rows) for j in range(2)]
    outs = list(take(1))
    (grad_one_ref,) = take(1)
    mixed_grad = take(grid_rows)
    first_grad, second_grad = take(2), take(2)
    act_ref, up_grad_ref, hidden_ref, down_grad_ref, attn_grad_ref, slope_ref, small = take(7)
    own_rows, half = dy[0].shape
    outs.append(second_grad[1].at[second_grad[1].shape[0] - own_rows :])
    width = 2 * half
    inner = mixed[0].shape[1] // 2
    rows = mixed[0].shape[0]
    part_hidden = first[0].shape[1]
    small[...] = jnp.zeros_like(small)

    def vector(index):
        row = plan["vectors"] + index
        return jnp.concatenate([second[0][row : row + 1, :], second[1][row : row + 1, :]], axis=1).astype(F32)

    output_bias, first_gain, first_shift, down_bias, second_gain, second_shift = (vector(i) for i in range(6))

    def mean(v):
        return jnp.sum(v, axis=1, keepdims=True) / width

    def norm(v):
        centred = v - mean(v)
        inverse = lax.rsqrt(mean(centred * centred) + EPSILON)
        return centred * inverse, inverse

    def norm_back(v, normed, inverse):
        return inverse * (v - mean(v) - normed * mean(v * normed))

    def total(v):
        return jnp.sum(v, axis=0, keepdims=True)

    def keep(row, v):
        small[row : row + 1, : v.shape[1]] += v

    for part in range(2):
        span = slice(part * rows, (part + 1) * rows)
        lanes = slice(part * inner, (part + 1) * inner)
        parts = []
        for j in range(2):
            parts.append(sum(nn(mixed[k][:, lanes], second[2 * k + j][plan["out"], :]) for k in range(grid_rows)))
        attention = jnp.concatenate(parts, axis=1) + output_bias
        normed_one, inverse_one = norm(x_ref[span, :].astype(F32) + attention)
        hidden = normed_one * first_gain + first_shift
        low = hidden.astype(BF)
        hidden_ref[span, :] = low
        downs = [jnp.zeros((rows, half), F32), jnp.zeros((rows, half), F32)]
        for k in range(grid_rows):
            cols = slice(k * part_hidden, (k + 1) * part_hidden)
            upward = nn(low[:, :half], first[2 * k][...]) + nn(low[:, half:], first[2 * k + 1][...])
            bias = [second[2 * k][plan["up_bias"] + u : plan["up_bias"] + u + 1, :] for u in range(part_hidden // half)]
            upward = upward + jnp.concatenate(bias, axis=1).astype(F32)
            bell = (1.0 + lax.erf(upward * (2.0**-0.5))) * 0.5
            slope_ref[:, cols] = bell + upward * jnp.exp(upward * upward * -0.5) * 0.3989422804014327
            act = (upward * bell).astype(BF)
            act_ref[span, cols] = act
            for j in range(2):
                downs[j] = downs[j] + nn(act, second[2 * k + j][plan["down"], :])
        downward = jnp.concatenate(downs, axis=1) + down_bias
        normed_two, inverse_two = norm(hidden + downward)
        final = (normed_two * second_gain + second_shift).astype(BF)
        outs[0][span, :] = final[:, :half]
        outs[1][span, :] = final[:, half:]
        grad_out = jnp.concatenate([dy[0][span, :], dy[1][span, :]], axis=1).astype(F32)
        keep(0, total(grad_out * normed_two))
        keep(1, total(grad_out))
        grad_two = norm_back(grad_out * second_gain, normed_two, inverse_two)
        down_grad = grad_two.astype(BF)
        down_grad_ref[span, :] = down_grad
        keep(4, total(down_grad.astype(F32)))
        grads = [grad_two[:, :half], grad_two[:, half:]]
        for k in range(grid_rows):
            cols = slice(k * part_hidden, (k + 1) * part_hidden)
            act_grad = nt(down_grad[:, :half], second[2 * k][plan["down"], :]) + nt(
                down_grad[:, half:], second[2 * k + 1][plan["down"], :]
            )
            up_grad = (act_grad * slope_ref[:, cols]).astype(BF)
            up_grad_ref[span, cols] = up_grad
            keep(8 + k, total(up_grad.astype(F32)))
            for j in range(2):
                grads[j] = grads[j] + nt(up_grad, first[2 * k + j][...])
        grad_hidden = jnp.concatenate(grads, axis=1)
        keep(2, total(grad_hidden * normed_one))
        keep(3, total(grad_hidden))
        grad_one = norm_back(grad_hidden * first_gain, normed_one, inverse_one)
        grad_one_ref[span, :] = grad_one
        attn_grad = grad_one.astype(BF)
        attn_grad_ref[span, :] = attn_grad
        keep(5, total(attn_grad.astype(F32)))
        for k in range(grid_rows):
            back = nt(attn_grad[:, :half], second[2 * k][plan["out"], :]) + nt(
                attn_grad[:, half:], second[2 * k + 1][plan["out"], :]
            )
            mixed_grad[k][:, lanes] = back.astype(BF)

    for j in range(2):
        side = slice(j * half, (j + 1) * half)
        for place, k in enumerate(plan["second_order"]):
            cols = slice(k * part_hidden, (k + 1) * part_hidden)
            grad = second_grad[j].at[place * plan["rows"] : (place + 1) * plan["rows"]]
            grad[plan["down"], :] = tn(act_ref[:, cols], down_grad_ref[:, side]).astype(BF)
            back = tn(mixed[k][:, :inner], attn_grad_ref[:rows, side])
            back = back + tn(mixed[k][:, inner:], attn_grad_ref[rows:, side])
            grad[plan["out"], :] = back.astype(BF)
            sums = [small[:6, side]] + [small[8 + k : 9 + k, u * half : (u + 1) * half] for u in range(part_hidden // half)]
            sums += [jnp.zeros((32 - 6 - part_hidden // half, half), F32)]
            grad[plan["sums"], :] = jnp.concatenate(sums, axis=0).astype(BF)
        for place, k in enumerate(plan["first_order"]):
            cols = slice(k * part_hidden, (k + 1) * part_hidden)
            first_grad[j][place, :, :] = tn(hidden_ref[:, side], up_grad_ref[:, cols]).astype(BF)


def input_grad_kernel(grid_rows, parts, where, *refs):
    pieces = [refs[i * grid_rows : (i + 1) * grid_rows] for i in range(parts)]
    weight, grad_one, own, other = refs[parts * grid_rows :]
    r, c = where[1], where[2]
    half = own.shape[1]
    rows = pieces[0][0].shape[0]
    for run in range(2):
        span = slice(run * rows, (run + 1) * rows)
        for j, out in enumerate((own, other)):
            total = grad_one[span, j * half : (j + 1) * half]
            for k in range(grid_rows):
                top = 0
                for part in pieces:
                    wide = part[k].shape[1] // 2
                    held = weight[(r ^ k) * 2 + (c ^ j), top : top + wide, :]
                    total = total + nn(part[k][:, run * wide : (run + 1) * wide], held)
                    top += wide
            out[span, :] = total.astype(BF)


def shift(array, axis, to):
    return lax.ppermute(array, axis, [(i, to(i)) for i in range(lax.axis_size(axis))])


def to_row(array, k):
    return shift(array, "row", lambda i: i ^ k)


def to_col(array):
    return shift(array, "col", lambda i: 1 - i)


def after(array, *earlier):
    return lax.optimization_barrier((array, *earlier))[0]


def gather_near(array):
    return to_row(array, 1), to_row(array, 2)


def gather_row(array, near, side, cut):
    got = [(0, 0, array), (1, 0, near), (2, 0, side), (3, 0, to_row(near[:cut], 2))]
    return got + ([(3, cut, to_row(side[cut:], 1))] if cut < array.shape[0] else [])


def after_all(arrays, *earlier):
    return lax.optimization_barrier((*arrays, *earlier))[: len(arrays)]


def add(*arrays):
    return sum(a.astype(F32) for a in arrays).astype(BF)


def reduce_first(own, got):
    return add(own[2:], got[2:])


def reduce_groups(array, group):
    if lax.axis_size("tok") != 4:
        return lax.psum(array, "tok")
    side = (group ^ (group >> 1)) & 1
    middle = array.shape[0] // 2
    low, high = array[:middle], array[middle:]
    half = add(jnp.where(side == 0, low, high), shift(jnp.where(side == 0, high, low), "tok", lambda i: i ^ 1))
    half = add(half, shift(half, "tok", lambda i: i ^ 3))
    rest = shift(half, "tok", lambda i: i ^ 1)
    return jnp.concatenate([jnp.where(side == 0, half, rest), jnp.where(side == 0, rest, half)], axis=0)


def local(
    tokens,
    cotangent,
    lengths,
    dealing,
    project_in,
    project_bias,
    project_out,
    output_bias,
    first_gain,
    first_shift,
    up_weight,
    up_bias,
    down_weight,
    down_bias,
    second_gain,
    second_shift,
):
    groups, grid_rows = lax.axis_size("tok"), lax.axis_size("row")
    group, row, col = lax.axis_index("tok"), lax.axis_index("row"), lax.axis_index("col")
    where = jnp.stack([group, row, col]).astype(jnp.int32)
    shard_rows, half = tokens.shape
    width = 2 * half
    count = dealing.shape[0] // (groups * grid_rows)
    block = shard_rows // count
    sizes = (groups, grid_rows, count, block)
    seqs = lengths.shape[1]
    inner = project_bias.shape[1]
    heads = inner // HEAD
    hidden_part = up_weight.shape[1]
    run = count // 4
    rows = run * block
    own_rows = shard_rows // 2
    half_rows = own_rows * grid_rows
    wide = 3 * inner
    per_pair = count // groups
    piece = (per_pair * block, half)
    shard = (shard_rows, half)
    both = pltpu.VMEM(shard, BF)

    def exchange(pieces):
        return [shift(p, "tok", lambda i, d=d: (i + d) % groups) if d else p for d, p in enumerate(pieces)]

    joined_weight = project_in.transpose(1, 2, 0).reshape(wide, half)
    out_rows = slice(hidden_part, hidden_part + inner)
    plan = {
        "down": slice(0, hidden_part),
        "out": out_rows,
        "vectors": out_rows.stop,
        "up_bias": out_rows.stop + 6,
        "sums": slice(out_rows.stop, out_rows.stop + 32),
        "rows": out_rows.stop + 32,
        "first_order": (0, 2, 1, 3),
        "second_order": (0, 1, 2, 3),
    }

    *sent, table = call(
        partial(send_kernel, sizes), [(piece, BF)] * groups + [((count + 8,), jnp.int32)], "ssv",
        out_spaces="v" * groups + "s",
    )(dealing, where, tokens)
    (place,) = call(partial(place_kernel, sizes), [((grid_rows * count,), jnp.int32)], "ss", [pltpu.SMEM((groups,), jnp.int32)], "s", 2)(
        dealing, where
    )
    got = exchange(sent)
    vectors = [output_bias, first_gain, first_shift, down_bias, second_gain, second_shift, up_bias]
    vectors = after(jnp.concatenate(vectors), *got).reshape(8, half)
    second_weights = jnp.concatenate(
        [after(down_weight, *got), after(project_out, *got), jnp.pad(vectors, ((0, 8), (0, 0)))], axis=0
    )
    first_near = gather_near(up_weight)
    chunk = jnp.concatenate(after_all(got, place, *first_near), axis=0)
    chunk_near = gather_near(chunk)
    dy_sent = call(partial(send_again_kernel, sizes), [(piece, BF)] * groups, "sv")(table, after(cotangent, *got))
    chunk_near = after_all(chunk_near, *dy_sent)
    layout, pieces = [], []
    parts = gather_row(chunk, *chunk_near, shard_rows // 2)
    for k, top, part in parts:
        layout += [(k, 0, top // block), (k, 1, top // block)]
        pieces += [part, to_col(part)]
    far = [part for k, _, part in parts if k == 3]
    second_all = lax.all_gather(after(second_weights, *chunk_near), ("row", "col"))
    first_row = after_all((up_weight, *first_near), *chunk_near)
    first_all = [part for weight in first_row for part in (weight, to_col(weight))]
    pieces[0] = after(pieces[0], *first_all)
    first_far = to_row(after(up_weight, *far), 3)
    dy_got = exchange(after_all(dy_sent, *far))
    wide_keys = 2 * rows
    q, k, v, kt, mixed_own, xq, x_own, *mixed = call(
        partial(attend_kernel, sizes, layout, heads, seqs, run),
        [
            ((heads, half_rows, LANES), BF),
            ((heads, 2 * half_rows, LANES), BF),
            ((heads, 2 * half_rows, LANES), BF),
            ((inner, 2 * half_rows), BF),
            ((heads, half_rows, HEAD), BF),
            ((half_rows, width), BF),
            ((own_rows, width), BF),
        ]
        + [((rows, 2 * inner), BF)] * grid_rows,
        "sss" + "v" * (len(pieces) + 3),
        [
            pltpu.VMEM((2 * half_rows, width), BF),
            pltpu.VMEM((heads, 2 * half_rows // wide_keys, rows, wide_keys), F32),
            pltpu.VMEM((heads, rows, LANES), F32),
            pltpu.VMEM((heads, rows, LANES), F32),
        ],
        us=47,
    )(place, where, lengths, *pieces, joined_weight, to_col(joined_weight), project_bias)

    mixed = after_all(mixed, *dy_got, first_far)
    first_far = after(first_far, mixed[0])
    first_all += [first_far, to_col(first_far)]
    dy_own, dy_other = call(
        partial(arrive_kernel, sizes, run), [((own_rows, half), BF)] * 2, "ss" + "v" * groups, [both]
    )(place, where, *dy_got)
    dy = [dy_own, to_col(dy_other)]

    def leave(own, other):
        return call(partial(return_kernel, sizes, run), [(piece, BF)] * groups, "ssvv", [both])(place, where, own, other)

    def come_back(pieces):
        return call(partial(final_kernel, sizes), [(shard, BF)], "s" + "v" * groups)(table, *pieces)[0]

    mixed_got = [to_row(m, i) if i else m for i, m in enumerate(mixed)]
    parts = ((0, heads - 1), (heads - 1, 1))
    held = [(i * heads + start) * HEAD for start, _ in parts for i in range(3)]
    spans = [number * HEAD for _, number in parts for _ in range(3)]
    split = jnp.concatenate([joined_weight[top : top + span] for top, span in zip(held, spans)], axis=0)
    joined_all = lax.all_gather(after(split, mixed[0]), ("row", "col"))
    hidden_all = grid_rows * hidden_part
    second_rows = plan["rows"]
    out0, grad_one, *rest = call(
        partial(middle_kernel, plan, grid_rows),
        [((own_rows, half), BF), ((own_rows, width), F32)]
        + [((rows, 2 * inner), BF)] * grid_rows
        + [((grid_rows, half, hidden_part), BF)] * 2
        + [((grid_rows * second_rows, half), BF), ((grid_rows * second_rows + own_rows, half), BF)],
        "s" + "v" * (grid_rows + 3 + 2 * grid_rows + 1),
        [
            pltpu.VMEM((own_rows, hidden_all), BF),
            pltpu.VMEM((own_rows, hidden_all), BF),
            pltpu.VMEM((own_rows, width), BF),
            pltpu.VMEM((own_rows, width), BF),
            pltpu.VMEM((own_rows, width), BF),
            pltpu.VMEM((rows, hidden_all), F32),
            pltpu.VMEM((16, width), F32),
        ],
        us=42,
    )(where, *mixed_got, x_own, *dy, *first_all, second_all)
    mixed_grad = rest[:grid_rows]
    first_own, first_other, second_own, second_other = rest[grid_rows:]
    mixed_grad_got = [to_row(m, i) if i else m for i, m in enumerate(mixed_grad)]
    first_got, second_got = to_col(first_other), to_col(second_other)
    out_pieces = leave(out0, second_got)
    first_leaving = add(first_own[2:], first_got[2:])
    second_cut = [slice(i * second_rows, (i + 1) * second_rows) for i in range(grid_rows)]
    second_far = slice(2 * second_rows, 4 * second_rows)
    second_leaving = add(second_own[second_far], second_got[second_far])
    first_leaving, second_leaving, *out_pieces = after_all((first_leaving, second_leaving, *out_pieces), *mixed_grad_got)
    first_came, second_came = to_row(first_leaving, 1), to_row(second_leaving, 2)
    out_got = exchange(out_pieces)
    mixed_grad_got[0] = after(mixed_grad_got[0], first_leaving, second_leaving, *out_pieces)

    def back(start, number, grads):
        held = {
            2: ((number, half_rows, LANES), start // number),
            3: ((number, 2 * half_rows, LANES), start // number),
            4: ((number, 2 * half_rows, LANES), start // number),
            5: ((number * HEAD, 2 * half_rows), start // number),
            6: ((number, half_rows, HEAD), start // number),
        }
        return call(
            partial(attend_back_kernel, grid_rows, heads, start, seqs, run, block),
            [
                ((number, half_rows, HEAD), BF),
                ((number, half_rows, LANES), F32),
                ((number, half_rows, LANES), BF),
            ],
            "ss" + "v" * (5 + grid_rows),
            [
                pltpu.VMEM((number, half_rows, LANES), BF),
                pltpu.VMEM((number, HEAD, rows), F32),
                pltpu.VMEM((number, 2 * half_rows, LANES), F32),
                pltpu.VMEM((number, 2 * half_rows, LANES), F32),
            ],
            us=16 * number,
            blocks=held,
        )(where, lengths, q, k, v, kt, mixed_own, *grads)

    def join(dq, own, got):
        number = dq.shape[0]
        *pieces, joined = call(
            partial(join_kernel, grid_rows),
            [((rows, 2 * number * 3 * HEAD), BF)] * grid_rows + [((half_rows, number * 3 * HEAD), BF)],
            "svvv",
            us=2 * number,
        )(where, dq, own, got)
        return [to_row(m, i) if i else m for i, m in enumerate(pieces)], pieces, joined

    dq, kv_own, kv_other = back(0, heads - 1, mixed_grad_got)
    kv_other = after(kv_other, first_came, second_came, *out_got)
    kv_got = to_col(kv_other)
    first_own, second_own, out_got[0] = after_all((first_own, second_own, out_got[0]), dq)
    first_parting = add(first_own[1], first_got[1], first_came[1])
    second_parting = add(second_own[second_cut[1]], second_got[second_cut[1]], second_came[second_rows:])
    first_last, second_last = to_row(first_parting, 2), to_row(second_parting, 1)
    joined_got, leaving, joined = join(dq, kv_own, kv_got)
    mixed_grad_got[0] = after(mixed_grad_got[0], first_parting, second_parting, *leaving)
    dq, kv_own, kv_other = back(heads - 1, 1, mixed_grad_got)
    kv_other = after(kv_other, first_last, second_last, *joined_got)
    first_own, second_own, out_got[0] = after_all((first_own, second_own, out_got[0]), dq)
    first_sum = add(first_own[0], first_got[0], first_came[0], first_last)
    second_sum = add(second_own[second_cut[0]], second_got[second_cut[0]], second_came[:second_rows], second_last)
    kv_got = after(to_col(kv_other), first_sum, second_sum)
    last_got, leaving, last_joined = join(dq, kv_own, kv_got)
    first_sum, second_sum = reduce_groups(first_sum, group), reduce_groups(second_sum, group)
    output = come_back(out_got)
    dx_own, dx_other = call(
        partial(input_grad_kernel, grid_rows, 2), [((own_rows, half), BF)] * 2, "s" + "v" * (2 * grid_rows + 2), us=7
    )(where, *joined_got, *last_got, joined_all, grad_one)
    dx_pieces = leave(dx_own, to_col(dx_other))
    in_own, in_other = call(project_in_grad_kernel, [((wide + 32, half), BF)] * 2, "vvv", us=6)(
        joined, after(last_joined, *dx_pieces), xq
    )
    in_sum = reduce_groups(add(in_own, to_col(in_other)), group)
    dx_got = exchange(dx_pieces)
    input_grad = come_back(dx_got)

    tops = [sum(spans[:i]) for i in range(6)]
    in_parts = [in_sum[top : top + span] for top, span in zip(tops, spans)]
    in_parts = [jnp.concatenate([in_parts[i], in_parts[3 + i]], axis=0) for i in range(3)]
    project_in_grad = jnp.stack(in_parts).transpose(2, 0, 1)
    sums = in_sum[wide : wide + 2].reshape(2 * half)
    in_sums = [sums[top : top + span] for top, span in zip(tops, spans)]
    sums = [jnp.concatenate([in_sums[i], in_sums[3 + i]]) for i in (0, 2)]
    tail = second_sum[plan["sums"]].astype(F32)
    return (
        output,
        input_grad,
        project_in_grad.astype(F32),
        jnp.stack(sums).astype(F32),
        second_sum[out_rows].astype(F32),
        tail[5],
        tail[2],
        tail[3],
        first_sum.astype(F32),
        tail[6:8].reshape(hidden_part),
        second_sum[:hidden_part].astype(F32),
        tail[4],
        tail[0],
        tail[1],
    )


def solution(mesh):
    stream, grid = P(("tok", "row"), "col"), P("row", "col")
    joined, mids, cols = P("col", None, "row"), P("col", "row"), P("col")
    in_specs = (
        stream, stream, P("tok", None), P(), joined, P(None, "row"), grid, cols,
        cols, cols, mids, P("row"), grid, cols, cols, cols,
    )
    out_specs = (
        stream, stream, joined, P(None, "row"), grid, cols,
        cols, cols, mids, P("row"), grid, cols, cols, cols,
    )
    return jax.shard_map(local, mesh=mesh, in_specs=in_specs, out_specs=out_specs, check_vma=False)
```

```python
from functools import partial

import jax
import jax.numpy as jnp
from jax import lax
from jax.experimental import pallas as pl
from jax.experimental.pallas import tpu as pltpu
from jax.sharding import PartitionSpec as P

HEAD = 64
LANES = 128
EPSILON = 1e-12
OFF = -1000000000.0
BF = jnp.bfloat16
F32 = jnp.float32
VMEM_LIMIT = 60 * 1024 * 1024


def nn(a, b):
    return lax.dot_general(a, b, (((1,), (0,)), ((), ())), preferred_element_type=F32)


def nt(a, b):
    return lax.dot_general(a, b, (((1,), (1,)), ((), ())), preferred_element_type=F32)


def tn(a, b):
    return lax.dot_general(a, b, (((0,), (0,)), ((), ())), preferred_element_type=F32)


def call(kernel, outs, spaces, scratch=(), out_spaces=None, us=2, blocks=()):
    memory = {"s": pltpu.SMEM, "v": pltpu.VMEM}
    specs = [pl.BlockSpec(memory_space=memory[s]) for s in spaces]
    for operand, (shape, index) in dict(blocks).items():
        specs[operand] = pl.BlockSpec(
            shape, lambda i, index=index, rank=len(shape): (index,) + (0,) * (rank - 1), pipeline_mode=pl.Buffered(1)
        )
    return pl.pallas_call(
        kernel,
        out_shape=[jax.ShapeDtypeStruct(shape, dtype) for shape, dtype in outs],
        grid=(1,) if blocks else (),
        in_specs=specs,
        out_specs=[pl.BlockSpec(memory_space=memory[s]) for s in out_spaces or "v" * len(outs)],
        scratch_shapes=list(scratch),
        compiler_params=pltpu.CompilerParams(vmem_limit_bytes=VMEM_LIMIT),
        cost_estimate=pl.CostEstimate(flops=us * 3 * 10**8, bytes_accessed=us * 10**6, transcendentals=0),
    )


def rows_at(block, size):
    return pl.ds(pl.multiple_of(block * size, size), size)


def send_kernel(sizes, deal, where, x, *outs):
    groups, grid_rows, count, block = sizes
    pieces, table = outs[:groups], outs[groups]
    per_pair = count // groups
    g, r = where[0], where[1]
    mine = g * grid_rows + r
    for d in range(groups):
        base = (lax.rem(g + d, groups) * grid_rows + r) * count

        def step(j, rank):
            source = deal[base + j]
            table[d * per_pair + rank] = lax.rem(source, count)
            return rank + (lax.div(source, count) == mine).astype(jnp.int32)

        lax.fori_loop(0, count, step, jnp.int32(0), unroll=8)
        for rank in range(per_pair):
            rows = rows_at(table[d * per_pair + rank], block)
            pieces[d][rank * block : (rank + 1) * block, :] = x[rows, :]


def send_again_kernel(sizes, table, x, *outs):
    groups, grid_rows, count, block = sizes
    per_pair = count // groups
    for d in range(groups):
        for rank in range(per_pair):
            rows = rows_at(table[d * per_pair + rank], block)
            outs[d][rank * block : (rank + 1) * block, :] = x[rows, :]


def final_kernel(sizes, table, *refs):
    groups, grid_rows, count, block = sizes
    pieces, out = refs[:groups], refs[groups]
    per_pair = count // groups
    for d in range(groups):
        for rank in range(per_pair):
            rows = rows_at(table[(groups - d) % groups * per_pair + rank], block)
            out[rows, :] = pieces[d][rank * block : (rank + 1) * block, :]


def place_kernel(sizes, deal, where, table, tally):
    groups, grid_rows, count, block = sizes
    per_pair = count // groups
    g, r = where[0], where[1]
    for k in range(grid_rows):
        base = (g * grid_rows + (r ^ k)) * count
        for d in range(groups):
            tally[d] = k * count + d * per_pair

        def step(j, carry):
            d = lax.rem(g - lax.div(deal[base + j], grid_rows * count) + groups, groups)
            at = tally[d]
            table[at] = j
            tally[d] = at + 1
            return carry

        lax.fori_loop(0, count, step, jnp.int32(0), unroll=8)


def home_of(j, run, c):
    turn = lax.div(j, run)
    other = (lax.rem(turn, 2) != c).astype(jnp.int32)
    return other * 2 * run + lax.div(turn, 2) * run + lax.rem(j, run)


def arrive_kernel(sizes, run, place, where, *refs):
    groups, grid_rows, count, block = sizes
    pieces, own, other, both = refs[:groups], refs[groups], refs[groups + 1], refs[groups + 2]
    per_pair = count // groups
    for d in range(groups):
        for rank in range(per_pair):
            at = home_of(place[d * per_pair + rank], run, where[2])
            both[rows_at(at, block), :] = pieces[d][rank * block : (rank + 1) * block, :]
    own[...] = both[: own.shape[0], :]
    other[...] = both[own.shape[0] :, :]


def return_kernel(sizes, run, place, where, own, other, *refs):
    groups, grid_rows, count, block = sizes
    outs, both = refs[:groups], refs[groups]
    per_pair = count // groups
    rows = own.shape[0]
    both[:rows, :] = own[...]
    both[rows:, :] = other[other.shape[0] - rows :, :]
    for d in range(groups):
        for rank in range(per_pair):
            at = home_of(place[(groups - d) % groups * per_pair + rank], run, where[2])
            outs[d][rank * block : (rank + 1) * block, :] = both[rows_at(at, block), :]


def sequence_ends(lengths, number):
    ends, total = [], jnp.int32(0)
    for s in range(number):
        total = total + lengths[0, s]
        ends.append(total)
    return ends


def sequence_of(ends, block):
    return sum((block >= end).astype(jnp.int32) for end in ends)


def first_of(ends, block):
    start = jnp.int32(0)
    for end in ends:
        start = jnp.where(block >= end, end, start)
    return start


def last_of(ends, block):
    stop = ends[-1]
    for end in reversed(ends):
        stop = jnp.where(block < end, end, stop)
    return stop


def key_steps(ends, first, run, block, wide, total):
    low = first_of(ends, first) * block
    steps = lax.div(last_of(ends, first + run - 1) * block - low + wide - 1, wide)
    low = jnp.minimum(low, total - steps * wide)
    return steps, lambda j: pl.ds(pl.multiple_of(low + j * wide, block), wide)


def thirds(v):
    one = v.astype(BF)
    rest = v - one.astype(F32)
    two = rest.astype(BF)
    three = (rest - two.astype(F32)).astype(BF)
    return one.astype(F32), two.astype(F32), three.astype(F32)


def attend_kernel(sizes, layout, heads, seqs, run, place, where, lengths, *refs):
    groups, grid_rows, count, block = sizes
    pieces = refs[: len(layout)]
    weights = refs[len(layout) : len(layout) + 2]
    bias = refs[len(layout) + 2]
    outs = refs[len(layout) + 3 :]
    q_ref, k_ref, v_ref, o_ref, xq_ref, own_ref = outs[:6]
    mixed = outs[6 : 6 + grid_rows]
    x_ref, score_ref, peak_ref, acc_ref = outs[6 + grid_rows :]
    r, c = where[1], where[2]
    ends = sequence_ends(lengths, seqs)
    half = weights[0].shape[1]
    inner = heads * HEAD
    rows = run * block
    for ref, (k, j, start) in zip(pieces, layout):
        for b in range(ref.shape[0] // block):
            at = (r ^ k) * count + place[k * count + start + b]
            x_ref[rows_at(at, block), j * half : (j + 1) * half] = ref[b * block : (b + 1) * block, :]
    local_runs = q_ref.shape[1] // rows
    shard_runs = local_runs // grid_rows
    lane = lax.broadcasted_iota(jnp.int32, (rows, HEAD), 1)
    down = lax.div(lax.broadcasted_iota(jnp.int32, (rows, HEAD), 0), block)
    ones_v = jnp.where(lane < 3, 1.0, 0.0)
    tail_k = (lane >= seqs) & (lane < seqs + 3)
    q_bias, v_bias = bias[0:1, :].astype(F32), bias[1:2, :].astype(F32)

    def project(i, mine):
        at = rows_at(i, rows)
        x0, x1 = x_ref[at, :half], x_ref[at, half:]
        first = 0 if mine else inner
        joined = nt(x0, weights[0][first:, :]) + nt(x1, weights[1][first:, :])
        seg = sequence_of(ends, down + i * run)
        key_tail = jnp.where((lane == seg) | tail_k, 1.0, 0.0)
        for h in range(heads):
            left = inner - first + h * HEAD
            value = joined[:, left + inner : left + inner + HEAD] + v_bias[:, h * HEAD : (h + 1) * HEAD]
            k_ref[h, at, :] = jnp.concatenate([joined[:, left : left + HEAD], key_tail], axis=1).astype(BF)
            v_ref[h, at, :] = jnp.concatenate([value, ones_v], axis=1).astype(BF)
        return at, joined, seg

    def pair(i, carry):
        project(2 * i + 1 - c, False)
        at, joined, seg = project(2 * i + c, True)
        here = rows_at(i, rows)
        query_tail = jnp.where((lane < seqs) & (lane != seg), OFF, 0.0)
        for h in range(heads):
            query = joined[:, h * HEAD : (h + 1) * HEAD] + q_bias[:, h * HEAD : (h + 1) * HEAD]
            query = query.astype(BF).astype(F32) * (HEAD**-0.5)
            q_ref[h, here, :] = jnp.concatenate([query, query_tail], axis=1).astype(BF)
        xq_ref[here, :] = x_ref[at, :]
        return carry

    lax.fori_loop(0, local_runs, pair, jnp.int32(0))
    own_ref[...] = xq_ref[rows_at(r, rows * shard_runs), :]
    wide = score_ref.shape[3]
    lane_q = lax.broadcasted_iota(jnp.int32, (rows, LANES), 1)

    def one_run(i, carry):
        steps, key_rows = key_steps(ends, i * 2 * run + c * run, run, block, wide, k_ref.shape[1])
        here = rows_at(i, rows)
        peak_ref[...] = jnp.full_like(peak_ref, -3e38)

        def score(j, state):
            for h in range(heads):
                scores = nt(q_ref[h, here, :], k_ref[h, key_rows(j), :])
                score_ref[h, j] = scores
                peak = peak_ref[h]
                for t in range(wide // LANES):
                    peak = jnp.maximum(peak, scores[:, t * LANES : (t + 1) * LANES])
                peak_ref[h] = peak
            return state

        lax.fori_loop(0, steps, score, jnp.int32(0))
        tops = [jnp.max(peak_ref[h], axis=1, keepdims=True) for h in range(heads)]
        for h in range(heads):
            peak_ref[h] = jnp.broadcast_to(tops[h], (rows, LANES))
        acc_ref[...] = jnp.zeros_like(acc_ref)

        def mix(j, state):
            for h in range(heads):
                peak = jnp.concatenate([peak_ref[h]] * (wide // LANES), axis=1)
                part = jnp.exp(score_ref[h, j] - peak).astype(BF)
                acc_ref[h] += nn(part, v_ref[h, key_rows(j), :])
            return state

        lax.fori_loop(0, steps, mix, jnp.int32(0))
        for h in range(heads):
            acc = acc_ref[h]
            total = acc[:, HEAD : HEAD + 1]
            o_ref[h, here, :] = (acc[:, :HEAD] / total).astype(BF)
            kept = q_ref[h, here, :].astype(F32)
            for t, term in enumerate(thirds(tops[h] + jnp.log(total))):
                kept = jnp.where(lane_q == HEAD + seqs + t, -term, kept)
            q_ref[h, here, :] = kept.astype(BF)
        return carry

    lax.fori_loop(0, local_runs, one_run, jnp.int32(0))
    for k in range(grid_rows):
        cells = [
            o_ref[h, rows_at((r ^ k) * shard_runs + part, rows), :] for part in range(shard_runs) for h in range(heads)
        ]
        mixed[k][...] = jnp.concatenate(cells, axis=1)


def attend_back_kernel(
    grid_rows, heads_all, start, seqs, run, block, where, lengths, q_ref, k_ref, v_ref, o_ref, *refs
):
    grads = refs[:grid_rows]
    dq_ref, own_ref, other_ref, do_ref, query_acc, key_acc, value_acc = refs[grid_rows:]
    r, c = where[1], where[2]
    heads = q_ref.shape[0]
    ends = sequence_ends(lengths, seqs)
    rows = run * block
    wide = 2 * rows
    local_runs = q_ref.shape[1] // rows
    shard_runs = local_runs // grid_rows
    lane = lax.broadcasted_iota(jnp.int32, (rows, HEAD), 1)
    for k in range(grid_rows):
        for part in range(shard_runs):
            at = rows_at((r ^ k) * shard_runs + part, rows)
            for h in range(heads):
                left = (part * heads_all + start + h) * HEAD
                grad = grads[k][:, left : left + HEAD].astype(F32)
                centre = jnp.sum(grad * o_ref[h, at, :].astype(F32), axis=1, keepdims=True)
                tail = jnp.zeros((rows, HEAD), F32)
                for t, term in enumerate(thirds(centre)):
                    tail = jnp.where(lane == t, -term, tail)
                do_ref[h, at, :] = jnp.concatenate([grad, tail], axis=1).astype(BF)
    key_acc[...] = jnp.zeros_like(key_acc)
    value_acc[...] = jnp.zeros_like(value_acc)

    def one_run(i, carry):
        steps, key_rows = key_steps(ends, i * 2 * run + c * run, run, block, wide, k_ref.shape[1])
        here = rows_at(i, rows)
        query_acc[...] = jnp.zeros_like(query_acc)

        def keys(j, state):
            at = key_rows(j)
            for h in range(heads):
                query, grad = q_ref[h, here, :], do_ref[h, here, :]
                key = k_ref[h, at, :]
                shares = jnp.exp(nt(key, query))
                score_grads = (shares * nt(v_ref[h, at, :], grad)).astype(BF)
                value_acc[h, at, :] += nn(shares.astype(BF), grad)
                key_acc[h, at, :] += nn(score_grads, query)
                query_acc[h] += tn(score_grads, key)
            return state

        lax.fori_loop(0, steps, keys, jnp.int32(0))
        for h in range(heads):
            dq_ref[h, here, :] = (query_acc[h, :, :HEAD] * (HEAD**-0.5)).astype(BF)
        return carry

    lax.fori_loop(0, local_runs, one_run, jnp.int32(0))

    def pair(i, carry):
        here = rows_at(i, rows)
        for h in range(heads):
            at = rows_at(2 * i + c, rows)
            own_ref[h, here, :] = jnp.concatenate([key_acc[h, at, :HEAD], value_acc[h, at, :HEAD]], axis=1)
            at = rows_at(2 * i + 1 - c, rows)
            other = jnp.concatenate([key_acc[h, at, :HEAD], value_acc[h, at, :HEAD]], axis=1)
            other_ref[h, here, :] = other.astype(BF)
        return carry

    lax.fori_loop(0, local_runs, pair, jnp.int32(0))


def join_kernel(grid_rows, where, dq_ref, own_ref, got_ref, *refs):
    pieces, joined = refs[:grid_rows], refs[grid_rows]
    r = where[1]
    heads, rows = dq_ref.shape[0], pieces[0].shape[0]
    shard_runs = pieces[0].shape[1] // joined.shape[1]
    for k in range(grid_rows):
        cells = []
        for part in range(shard_runs):
            at = rows_at((r ^ k) * shard_runs + part, rows)
            both = [(own_ref[h, at, :] + got_ref[h, at, :].astype(F32)).astype(BF) for h in range(heads)]
            mine = [dq_ref[h, at, :] for h in range(heads)]
            mine += [b[:, :HEAD] for b in both] + [b[:, HEAD:] for b in both]
            joined[at, :] = jnp.concatenate(mine, axis=1)
            cells += mine
        pieces[k][...] = jnp.concatenate(cells, axis=1)


def project_in_grad_kernel(*refs):
    joined, (xq, own, other) = refs[:-3], refs[-3:]
    half = own.shape[1]
    top, totals = 0, []
    for part in joined:
        wide = part.shape[1]
        own[top : top + wide, :] = tn(part[...], xq[:, :half]).astype(BF)
        other[top : top + wide, :] = tn(part[...], xq[:, half:]).astype(BF)
        totals.append(jnp.sum(part[...].astype(F32), axis=0, keepdims=True))
        top += wide
    total = jnp.concatenate([*totals, jnp.zeros((1, 2 * half - top), F32)], axis=1)
    below = own.shape[0] - top
    sums = jnp.concatenate([total[:, :half], total[:, half:], jnp.zeros((below - 2, half), F32)], axis=0).astype(BF)
    own[top:, :] = sums
    other[top:, :] = sums


def middle_kernel(plan, grid_rows, where, *refs):
    at = 0

    def take(n):
        nonlocal at
        got = refs[at : at + n]
        at += n
        return got

    r, c = where[1], where[2]
    mixed = take(grid_rows)
    (x_ref,) = take(1)
    dy = take(2)
    first = take(2 * grid_rows)
    (gathered,) = take(1)
    second = [gathered.at[(r ^ k) * 2 + (c ^ j)] for k in range(grid_rows) for j in range(2)]
    outs = list(take(1))
    (grad_one_ref,) = take(1)
    mixed_grad = take(grid_rows)
    first_grad, second_grad = take(2), take(2)
    act_ref, up_grad_ref, hidden_ref, down_grad_ref, attn_grad_ref, slope_ref, small = take(7)
    own_rows, half = dy[0].shape
    outs.append(second_grad[1].at[second_grad[1].shape[0] - own_rows :])
    width = 2 * half
    inner = mixed[0].shape[1] // 2
    rows = mixed[0].shape[0]
    part_hidden = first[0].shape[1]
    small[...] = jnp.zeros_like(small)

    def vector(index):
        row = plan["vectors"] + index
        return jnp.concatenate([second[0][row : row + 1, :], second[1][row : row + 1, :]], axis=1).astype(F32)

    output_bias, first_gain, first_shift, down_bias, second_gain, second_shift = (vector(i) for i in range(6))

    def mean(v):
        return jnp.sum(v, axis=1, keepdims=True) / width

    def norm(v):
        centred = v - mean(v)
        inverse = lax.rsqrt(mean(centred * centred) + EPSILON)
        return centred * inverse, inverse

    def norm_back(v, normed, inverse):
        return inverse * (v - mean(v) - normed * mean(v * normed))

    def total(v):
        return jnp.sum(v, axis=0, keepdims=True)

    def keep(row, v):
        small[row : row + 1, : v.shape[1]] += v

    for part in range(2):
        span = slice(part * rows, (part + 1) * rows)
        lanes = slice(part * inner, (part + 1) * inner)
        parts = []
        for j in range(2):
            parts.append(sum(nn(mixed[k][:, lanes], second[2 * k + j][plan["out"], :]) for k in range(grid_rows)))
        attention = jnp.concatenate(parts, axis=1) + output_bias
        normed_one, inverse_one = norm(x_ref[span, :].astype(F32) + attention)
        hidden = normed_one * first_gain + first_shift
        low = hidden.astype(BF)
        hidden_ref[span, :] = low
        downs = [jnp.zeros((rows, half), F32), jnp.zeros((rows, half), F32)]
        for k in range(grid_rows):
            cols = slice(k * part_hidden, (k + 1) * part_hidden)
            upward = nn(low[:, :half], first[2 * k][...]) + nn(low[:, half:], first[2 * k + 1][...])
            bias = [second[2 * k][plan["up_bias"] + u : plan["up_bias"] + u + 1, :] for u in range(part_hidden // half)]
            upward = upward + jnp.concatenate(bias, axis=1).astype(F32)
            bell = (1.0 + lax.erf(upward * (2.0**-0.5))) * 0.5
            slope_ref[:, cols] = bell + upward * jnp.exp(upward * upward * -0.5) * 0.3989422804014327
            act = (upward * bell).astype(BF)
            act_ref[span, cols] = act
            for j in range(2):
                downs[j] = downs[j] + nn(act, second[2 * k + j][plan["down"], :])
        downward = jnp.concatenate(downs, axis=1) + down_bias
        normed_two, inverse_two = norm(hidden + downward)
        final = (normed_two * second_gain + second_shift).astype(BF)
        outs[0][span, :] = final[:, :half]
        outs[1][span, :] = final[:, half:]
        grad_out = jnp.concatenate([dy[0][span, :], dy[1][span, :]], axis=1).astype(F32)
        keep(0, total(grad_out * normed_two))
        keep(1, total(grad_out))
        grad_two = norm_back(grad_out * second_gain, normed_two, inverse_two)
        down_grad = grad_two.astype(BF)
        down_grad_ref[span, :] = down_grad
        keep(4, total(down_grad.astype(F32)))
        grads = [grad_two[:, :half], grad_two[:, half:]]
        for k in range(grid_rows):
            cols = slice(k * part_hidden, (k + 1) * part_hidden)
            act_grad = nt(down_grad[:, :half], second[2 * k][plan["down"], :]) + nt(
                down_grad[:, half:], second[2 * k + 1][plan["down"], :]
            )
            up_grad = (act_grad * slope_ref[:, cols]).astype(BF)
            up_grad_ref[span, cols] = up_grad
            keep(8 + k, total(up_grad.astype(F32)))
            for j in range(2):
                grads[j] = grads[j] + nt(up_grad, first[2 * k + j][...])
        grad_hidden = jnp.concatenate(grads, axis=1)
        keep(2, total(grad_hidden * normed_one))
        keep(3, total(grad_hidden))
        grad_one = norm_back(grad_hidden * first_gain, normed_one, inverse_one)
        grad_one_ref[span, :] = grad_one
        attn_grad = grad_one.astype(BF)
        attn_grad_ref[span, :] = attn_grad
        keep(5, total(attn_grad.astype(F32)))
        for k in range(grid_rows):
            back = nt(attn_grad[:, :half], second[2 * k][plan["out"], :]) + nt(
                attn_grad[:, half:], second[2 * k + 1][plan["out"], :]
            )
            mixed_grad[k][:, lanes] = back.astype(BF)

    for j in range(2):
        side = slice(j * half, (j + 1) * half)
        for place, k in enumerate(plan["second_order"]):
            cols = slice(k * part_hidden, (k + 1) * part_hidden)
            grad = second_grad[j].at[place * plan["rows"] : (place + 1) * plan["rows"]]
            grad[plan["down"], :] = tn(act_ref[:, cols], down_grad_ref[:, side]).astype(BF)
            back = tn(mixed[k][:, :inner], attn_grad_ref[:rows, side])
            back = back + tn(mixed[k][:, inner:], attn_grad_ref[rows:, side])
            grad[plan["out"], :] = back.astype(BF)
            sums = [small[:6, side]] + [small[8 + k : 9 + k, u * half : (u + 1) * half] for u in range(part_hidden // half)]
            sums += [jnp.zeros((32 - 6 - part_hidden // half, half), F32)]
            grad[plan["sums"], :] = jnp.concatenate(sums, axis=0).astype(BF)
        for place, k in enumerate(plan["first_order"]):
            cols = slice(k * part_hidden, (k + 1) * part_hidden)
            first_grad[j][place, :, :] = tn(hidden_ref[:, side], up_grad_ref[:, cols]).astype(BF)


def input_grad_kernel(grid_rows, parts, where, *refs):
    pieces = [refs[i * grid_rows : (i + 1) * grid_rows] for i in range(parts)]
    weight, grad_one, own, other = refs[parts * grid_rows :]
    r, c = where[1], where[2]
    half = own.shape[1]
    rows = pieces[0][0].shape[0]
    for run in range(2):
        span = slice(run * rows, (run + 1) * rows)
        for j, out in enumerate((own, other)):
            total = grad_one[span, j * half : (j + 1) * half]
            for k in range(grid_rows):
                top = 0
                for part in pieces:
                    wide = part[k].shape[1] // 2
                    held = weight[(r ^ k) * 2 + (c ^ j), top : top + wide, :]
                    total = total + nn(part[k][:, run * wide : (run + 1) * wide], held)
                    top += wide
            out[span, :] = total.astype(BF)


def shift(array, axis, to):
    return lax.ppermute(array, axis, [(i, to(i)) for i in range(lax.axis_size(axis))])


def to_row(array, k):
    return shift(array, "row", lambda i: i ^ k)


def to_col(array):
    return shift(array, "col", lambda i: 1 - i)


def after(array, *earlier):
    return lax.optimization_barrier((array, *earlier))[0]


def gather_near(array):
    return to_row(array, 1), to_row(array, 2)


def gather_row(array, near, side, cut):
    got = [(0, 0, array), (1, 0, near), (2, 0, side), (3, 0, to_row(near[:cut], 2))]
    return got + ([(3, cut, to_row(side[cut:], 1))] if cut < array.shape[0] else [])


def after_all(arrays, *earlier):
    return lax.optimization_barrier((*arrays, *earlier))[: len(arrays)]


def add(*arrays):
    return sum(a.astype(F32) for a in arrays).astype(BF)


def reduce_first(own, got):
    return add(own[2:], got[2:])


def reduce_groups(array, group, second=(), third=()):
    if lax.axis_size("tok") != 4:
        return lax.psum(array, "tok")
    side = (group ^ (group >> 1)) & 1
    middle = array.shape[0] // 2
    low, high = array[:middle], array[middle:]
    half = add(jnp.where(side == 0, low, high), shift(jnp.where(side == 0, high, low), "tok", lambda i: i ^ 1))
    half = after(half, *second)
    half = add(after(half, *third), shift(half, "tok", lambda i: i ^ 3))
    rest = shift(half, "tok", lambda i: i ^ 1)
    return jnp.concatenate([jnp.where(side == 0, half, rest), jnp.where(side == 0, rest, half)], axis=0)


def local(
    tokens,
    cotangent,
    lengths,
    dealing,
    project_in,
    project_bias,
    project_out,
    output_bias,
    first_gain,
    first_shift,
    up_weight,
    up_bias,
    down_weight,
    down_bias,
    second_gain,
    second_shift,
):
    groups, grid_rows = lax.axis_size("tok"), lax.axis_size("row")
    group, row, col = lax.axis_index("tok"), lax.axis_index("row"), lax.axis_index("col")
    where = jnp.stack([group, row, col]).astype(jnp.int32)
    shard_rows, half = tokens.shape
    width = 2 * half
    count = dealing.shape[0] // (groups * grid_rows)
    block = shard_rows // count
    sizes = (groups, grid_rows, count, block)
    seqs = lengths.shape[1]
    inner = project_bias.shape[1]
    heads = inner // HEAD
    hidden_part = up_weight.shape[1]
    run = count // 4
    rows = run * block
    own_rows = shard_rows // 2
    half_rows = own_rows * grid_rows
    wide = 3 * inner
    per_pair = count // groups
    piece = (per_pair * block, half)
    shard = (shard_rows, half)
    both = pltpu.VMEM(shard, BF)

    def exchange(pieces):
        return [shift(p, "tok", lambda i, d=d: (i + d) % groups) if d else p for d, p in enumerate(pieces)]

    joined_weight = project_in.transpose(1, 2, 0).reshape(wide, half)
    out_rows = slice(hidden_part, hidden_part + inner)
    plan = {
        "down": slice(0, hidden_part),
        "out": out_rows,
        "vectors": out_rows.stop,
        "up_bias": out_rows.stop + 6,
        "sums": slice(out_rows.stop, out_rows.stop + 32),
        "rows": out_rows.stop + 32,
        "first_order": (0, 2, 1, 3),
        "second_order": (0, 1, 2, 3),
    }

    *sent, table = call(
        partial(send_kernel, sizes), [(piece, BF)] * groups + [((count + 8,), jnp.int32)], "ssv",
        out_spaces="v" * groups + "s",
    )(dealing, where, tokens)
    (place,) = call(partial(place_kernel, sizes), [((grid_rows * count,), jnp.int32)], "ss", [pltpu.SMEM((groups,), jnp.int32)], "s", 2)(
        dealing, where
    )
    got = exchange(sent)
    vectors = [output_bias, first_gain, first_shift, down_bias, second_gain, second_shift, up_bias]
    vectors = after(jnp.concatenate(vectors), *got).reshape(8, half)
    second_weights = jnp.concatenate(
        [after(down_weight, *got), after(project_out, *got), jnp.pad(vectors, ((0, 8), (0, 0)))], axis=0
    )
    first_near = gather_near(up_weight)
    chunk = jnp.concatenate(after_all(got, place, *first_near), axis=0)
    chunk_near = gather_near(chunk)
    dy_sent = call(partial(send_again_kernel, sizes), [(piece, BF)] * groups, "sv")(table, after(cotangent, *got))
    dy_got = exchange(dy_sent)
    chunk_near = after_all(chunk_near, *dy_got)
    layout, pieces = [], []
    parts = gather_row(chunk, *chunk_near, shard_rows // 2)
    for k, top, part in parts:
        layout += [(k, 0, top // block), (k, 1, top // block)]
        pieces += [part, to_col(part)]
    far = [part for k, _, part in parts if k == 3]
    second_all = lax.all_gather(after(second_weights, *chunk_near), ("row", "col"))
    first_row = after_all((up_weight, *first_near), *chunk_near)
    first_all = [part for weight in first_row for part in (weight, to_col(weight))]
    pieces[0] = after(pieces[0], *first_all)
    first_far = to_row(after(up_weight, *far), 3)
    wide_keys = 2 * rows
    q, k, v, mixed_own, xq, x_own, *mixed = call(
        partial(attend_kernel, sizes, layout, heads, seqs, run),
        [
            ((heads, half_rows, LANES), BF),
            ((heads, 2 * half_rows, LANES), BF),
            ((heads, 2 * half_rows, LANES), BF),
            ((heads, half_rows, HEAD), BF),
            ((half_rows, width), BF),
            ((own_rows, width), BF),
        ]
        + [((rows, 2 * inner), BF)] * grid_rows,
        "sss" + "v" * (len(pieces) + 3),
        [
            pltpu.VMEM((2 * half_rows, width), BF),
            pltpu.VMEM((heads, 2 * half_rows // wide_keys, rows, wide_keys), F32),
            pltpu.VMEM((heads, rows, LANES), F32),
            pltpu.VMEM((heads, rows, LANES), F32),
        ],
        us=47,
    )(place, where, lengths, *pieces, joined_weight, to_col(joined_weight), project_bias)

    mixed = after_all(mixed, first_far)
    dy_got[0] = after(dy_got[0], mixed[0])
    first_far = after(first_far, mixed[0])
    first_all += [first_far, to_col(first_far)]
    dy_own, dy_other = call(
        partial(arrive_kernel, sizes, run), [((own_rows, half), BF)] * 2, "ss" + "v" * groups, [both]
    )(place, where, *dy_got)
    dy = [dy_own, to_col(dy_other)]

    def leave(own, other):
        return call(partial(return_kernel, sizes, run), [(piece, BF)] * groups, "ssvv", [both])(place, where, own, other)

    def come_back(pieces):
        return call(partial(final_kernel, sizes), [(shard, BF)], "s" + "v" * groups)(table, *pieces)[0]

    mixed_got = [to_row(m, i) if i else m for i, m in enumerate(mixed)]
    parts = ((0, heads - 1), (heads - 1, 1))
    held = [(i * heads + start) * HEAD for start, _ in parts for i in range(3)]
    spans = [number * HEAD for _, number in parts for _ in range(3)]
    split = jnp.concatenate([joined_weight[top : top + span] for top, span in zip(held, spans)], axis=0)
    joined_all = lax.all_gather(after(split, mixed[0]), ("row", "col"))
    hidden_all = grid_rows * hidden_part
    second_rows = plan["rows"]
    out0, grad_one, *rest = call(
        partial(middle_kernel, plan, grid_rows),
        [((own_rows, half), BF), ((own_rows, width), F32)]
        + [((rows, 2 * inner), BF)] * grid_rows
        + [((grid_rows, half, hidden_part), BF)] * 2
        + [((grid_rows * second_rows, half), BF), ((grid_rows * second_rows + own_rows, half), BF)],
        "s" + "v" * (grid_rows + 3 + 2 * grid_rows + 1),
        [
            pltpu.VMEM((own_rows, hidden_all), BF),
            pltpu.VMEM((own_rows, hidden_all), BF),
            pltpu.VMEM((own_rows, width), BF),
            pltpu.VMEM((own_rows, width), BF),
            pltpu.VMEM((own_rows, width), BF),
            pltpu.VMEM((rows, hidden_all), F32),
            pltpu.VMEM((16, width), F32),
        ],
        us=42,
    )(where, *mixed_got, x_own, *dy, *first_all, second_all)
    mixed_grad = rest[:grid_rows]
    first_own, first_other, second_own, second_other = rest[grid_rows:]
    mixed_grad_got = [to_row(m, i) if i else m for i, m in enumerate(mixed_grad)]
    first_got, second_got = to_col(first_other), to_col(second_other)
    out_pieces = leave(out0, second_got)
    first_leaving = add(first_own[2:], first_got[2:])
    second_cut = [slice(i * second_rows, (i + 1) * second_rows) for i in range(grid_rows)]
    second_far = slice(2 * second_rows, 4 * second_rows)
    second_leaving = add(second_own[second_far], second_got[second_far])
    first_leaving, second_leaving, *out_pieces = after_all((first_leaving, second_leaving, *out_pieces), *mixed_grad_got)
    first_came, second_came = to_row(first_leaving, 1), to_row(second_leaving, 2)
    out_got = exchange(out_pieces)
    mixed_grad_got[0] = after(mixed_grad_got[0], first_leaving, second_leaving, *out_pieces)

    def back(start, number, grads):
        held = {
            2: ((number, half_rows, LANES), start // number),
            3: ((number, 2 * half_rows, LANES), start // number),
            4: ((number, 2 * half_rows, LANES), start // number),
            5: ((number, half_rows, HEAD), start // number),
        }
        return call(
            partial(attend_back_kernel, grid_rows, heads, start, seqs, run, block),
            [
                ((number, half_rows, HEAD), BF),
                ((number, half_rows, LANES), F32),
                ((number, half_rows, LANES), BF),
            ],
            "ss" + "v" * (4 + grid_rows),
            [
                pltpu.VMEM((number, half_rows, LANES), BF),
                pltpu.VMEM((number, rows, LANES), F32),
                pltpu.VMEM((number, 2 * half_rows, LANES), F32),
                pltpu.VMEM((number, 2 * half_rows, LANES), F32),
            ],
            us=16 * number,
            blocks=held,
        )(where, lengths, q, k, v, mixed_own, *grads)

    def join(dq, own, got):
        number = dq.shape[0]
        *pieces, joined = call(
            partial(join_kernel, grid_rows),
            [((rows, 2 * number * 3 * HEAD), BF)] * grid_rows + [((half_rows, number * 3 * HEAD), BF)],
            "svvv",
            us=2 * number,
        )(where, dq, own, got)
        return [to_row(m, i) if i else m for i, m in enumerate(pieces)], pieces, joined

    dq, kv_own, kv_other = back(0, heads - 1, mixed_grad_got)
    kv_other = after(kv_other, first_came, second_came, *out_got)
    kv_got = to_col(kv_other)
    first_own, second_own, out_got[0] = after_all((first_own, second_own, out_got[0]), dq)
    first_parting = add(first_own[1], first_got[1], first_came[1])
    second_parting = add(second_own[second_cut[1]], second_got[second_cut[1]], second_came[second_rows:])
    first_last, second_last = to_row(first_parting, 2), to_row(second_parting, 1)
    joined_got, leaving, joined = join(dq, kv_own, kv_got)
    mixed_grad_got[0] = after(mixed_grad_got[0], first_parting, second_parting, *leaving)
    dq, kv_own, kv_other = back(heads - 1, 1, mixed_grad_got)
    kv_other = after(kv_other, first_last, second_last, *joined_got)
    first_own, second_own, out_got[0] = after_all((first_own, second_own, out_got[0]), dq)
    first_sum = add(first_own[0], first_got[0], first_came[0], first_last)
    second_sum = add(second_own[second_cut[0]], second_got[second_cut[0]], second_came[:second_rows], second_last)
    kv_got = after(to_col(kv_other), first_sum, second_sum)
    last_got, leaving, last_joined = join(dq, kv_own, kv_got)
    output = come_back(out_got)
    in_own, in_other = call(project_in_grad_kernel, [((wide + 32, half), BF)] * 2, "vvv", us=6)(joined, last_joined, xq)
    in_got = to_col(in_other)
    last_got[0] = after(last_got[0], in_own)
    dx_own, dx_other = call(
        partial(input_grad_kernel, grid_rows, 2), [((own_rows, half), BF)] * 2, "s" + "v" * (2 * grid_rows + 2), us=7
    )(where, *joined_got, *last_got, joined_all, grad_one)
    dx_pieces = leave(dx_own, to_col(dx_other))
    first_sum = reduce_groups(first_sum, group, (last_joined,), dx_pieces)
    second_sum = reduce_groups(second_sum, group, (last_joined,), dx_pieces)
    dx_got = exchange(dx_pieces)
    input_grad = come_back(dx_got)
    in_sum = reduce_groups(add(in_own, in_got), group, dx_pieces)

    tops = [sum(spans[:i]) for i in range(6)]
    in_parts = [in_sum[top : top + span] for top, span in zip(tops, spans)]
    in_parts = [jnp.concatenate([in_parts[i], in_parts[3 + i]], axis=0) for i in range(3)]
    project_in_grad = jnp.stack(in_parts).transpose(2, 0, 1)
    sums = in_sum[wide : wide + 2].reshape(2 * half)
    in_sums = [sums[top : top + span] for top, span in zip(tops, spans)]
    sums = [jnp.concatenate([in_sums[i], in_sums[3 + i]]) for i in (0, 2)]
    tail = second_sum[plan["sums"]].astype(F32)
    return (
        output,
        input_grad,
        project_in_grad.astype(F32),
        jnp.stack(sums).astype(F32),
        second_sum[out_rows].astype(F32),
        tail[5],
        tail[2],
        tail[3],
        first_sum.astype(F32),
        tail[6:8].reshape(hidden_part),
        second_sum[:hidden_part].astype(F32),
        tail[4],
        tail[0],
        tail[1],
    )


def solution(mesh):
    stream, grid = P(("tok", "row"), "col"), P("row", "col")
    joined, mids, cols = P("col", None, "row"), P("col", "row"), P("col")
    in_specs = (
        stream, stream, P("tok", None), P(), joined, P(None, "row"), grid, cols,
        cols, cols, mids, P("row"), grid, cols, cols, cols,
    )
    out_specs = (
        stream, stream, joined, P(None, "row"), grid, cols,
        cols, cols, mids, P("row"), grid, cols, cols, cols,
    )
    return jax.shard_map(local, mesh=mesh, in_specs=in_specs, out_specs=out_specs, check_vma=False)
```

```python
from functools import partial

import jax
import jax.numpy as jnp
from jax import lax
from jax.experimental import pallas as pl
from jax.experimental.pallas import tpu as pltpu
from jax.sharding import PartitionSpec as P

HEAD = 64
LANES = 128
EPSILON = 1e-12
OFF = -1000000000.0
BF = jnp.bfloat16
F32 = jnp.float32
VMEM_LIMIT = 60 * 1024 * 1024


def nn(a, b):
    return lax.dot_general(a, b, (((1,), (0,)), ((), ())), preferred_element_type=F32)


def nt(a, b):
    return lax.dot_general(a, b, (((1,), (1,)), ((), ())), preferred_element_type=F32)


def tn(a, b):
    return lax.dot_general(a, b, (((0,), (0,)), ((), ())), preferred_element_type=F32)


def call(kernel, outs, spaces, scratch=(), out_spaces=None, us=2, blocks=()):
    memory = {"s": pltpu.SMEM, "v": pltpu.VMEM}
    specs = [pl.BlockSpec(memory_space=memory[s]) for s in spaces]
    for operand, (shape, index) in dict(blocks).items():
        specs[operand] = pl.BlockSpec(
            shape, lambda i, index=index, rank=len(shape): (index,) + (0,) * (rank - 1), pipeline_mode=pl.Buffered(1)
        )
    return pl.pallas_call(
        kernel,
        out_shape=[jax.ShapeDtypeStruct(shape, dtype) for shape, dtype in outs],
        grid=(1,) if blocks else (),
        in_specs=specs,
        out_specs=[pl.BlockSpec(memory_space=memory[s]) for s in out_spaces or "v" * len(outs)],
        scratch_shapes=list(scratch),
        compiler_params=pltpu.CompilerParams(vmem_limit_bytes=VMEM_LIMIT),
        cost_estimate=pl.CostEstimate(flops=us * 3 * 10**8, bytes_accessed=us * 10**6, transcendentals=0),
    )


def rows_at(block, size):
    return pl.ds(pl.multiple_of(block * size, size), size)


def send_kernel(sizes, deal, where, x, *outs):
    groups, grid_rows, count, block = sizes
    pieces, table = outs[:groups], outs[groups]
    per_pair = count // groups
    g, r = where[0], where[1]
    mine = g * grid_rows + r
    for d in range(groups):
        base = (lax.rem(g + d, groups) * grid_rows + r) * count

        def step(j, rank):
            source = deal[base + j]
            table[d * per_pair + rank] = lax.rem(source, count)
            return rank + (lax.div(source, count) == mine).astype(jnp.int32)

        lax.fori_loop(0, count, step, jnp.int32(0), unroll=8)
        for rank in range(per_pair):
            rows = rows_at(table[d * per_pair + rank], block)
            pieces[d][rank * block : (rank + 1) * block, :] = x[rows, :]


def send_again_kernel(sizes, table, x, *outs):
    groups, grid_rows, count, block = sizes
    per_pair = count // groups
    for d in range(groups):
        for rank in range(per_pair):
            rows = rows_at(table[d * per_pair + rank], block)
            outs[d][rank * block : (rank + 1) * block, :] = x[rows, :]


def final_kernel(sizes, table, *refs):
    groups, grid_rows, count, block = sizes
    pieces, out = refs[:groups], refs[groups]
    per_pair = count // groups
    for d in range(groups):
        for rank in range(per_pair):
            rows = rows_at(table[(groups - d) % groups * per_pair + rank], block)
            out[rows, :] = pieces[d][rank * block : (rank + 1) * block, :]


def place_kernel(sizes, deal, where, table, tally):
    groups, grid_rows, count, block = sizes
    per_pair = count // groups
    g, r = where[0], where[1]
    for k in range(grid_rows):
        base = (g * grid_rows + (r ^ k)) * count
        for d in range(groups):
            tally[d] = k * count + d * per_pair

        def step(j, carry):
            d = lax.rem(g - lax.div(deal[base + j], grid_rows * count) + groups, groups)
            at = tally[d]
            table[at] = j
            tally[d] = at + 1
            return carry

        lax.fori_loop(0, count, step, jnp.int32(0), unroll=8)


def home_of(j, run, c):
    turn = lax.div(j, run)
    other = (lax.rem(turn, 2) != c).astype(jnp.int32)
    return other * 2 * run + lax.div(turn, 2) * run + lax.rem(j, run)


def arrive_kernel(sizes, run, place, where, *refs):
    groups, grid_rows, count, block = sizes
    pieces, own, other, both = refs[:groups], refs[groups], refs[groups + 1], refs[groups + 2]
    per_pair = count // groups
    for d in range(groups):
        for rank in range(per_pair):
            at = home_of(place[d * per_pair + rank], run, where[2])
            both[rows_at(at, block), :] = pieces[d][rank * block : (rank + 1) * block, :]
    own[...] = both[: own.shape[0], :]
    other[...] = both[own.shape[0] :, :]


def return_kernel(sizes, run, place, where, own, other, *refs):
    groups, grid_rows, count, block = sizes
    outs, both = refs[:groups], refs[groups]
    per_pair = count // groups
    rows = own.shape[0]
    both[:rows, :] = own[...]
    both[rows:, :] = other[other.shape[0] - rows :, :]
    for d in range(groups):
        for rank in range(per_pair):
            at = home_of(place[(groups - d) % groups * per_pair + rank], run, where[2])
            outs[d][rank * block : (rank + 1) * block, :] = both[rows_at(at, block), :]


def sequence_ends(lengths, number):
    ends, total = [], jnp.int32(0)
    for s in range(number):
        total = total + lengths[0, s]
        ends.append(total)
    return ends


def sequence_of(ends, block):
    return sum((block >= end).astype(jnp.int32) for end in ends)


def first_of(ends, block):
    start = jnp.int32(0)
    for end in ends:
        start = jnp.where(block >= end, end, start)
    return start


def last_of(ends, block):
    stop = ends[-1]
    for end in reversed(ends):
        stop = jnp.where(block < end, end, stop)
    return stop


def key_steps(ends, first, run, block, wide, total):
    low = first_of(ends, first) * block
    steps = lax.div(last_of(ends, first + run - 1) * block - low + wide - 1, wide)
    low = jnp.minimum(low, total - steps * wide)
    return steps, lambda j: pl.ds(pl.multiple_of(low + j * wide, block), wide)


def thirds(v):
    one = v.astype(BF)
    rest = v - one.astype(F32)
    two = rest.astype(BF)
    three = (rest - two.astype(F32)).astype(BF)
    return one.astype(F32), two.astype(F32), three.astype(F32)


def attend_kernel(sizes, layout, heads, seqs, run, place, where, lengths, *refs):
    groups, grid_rows, count, block = sizes
    pieces = refs[: len(layout)]
    weights = refs[len(layout) : len(layout) + 2]
    bias = refs[len(layout) + 2]
    outs = refs[len(layout) + 3 :]
    q_ref, k_ref, v_ref, o_ref, xq_ref, own_ref = outs[:6]
    mixed = outs[6 : 6 + grid_rows]
    x_ref, score_ref, peak_ref, acc_ref = outs[6 + grid_rows :]
    r, c = where[1], where[2]
    ends = sequence_ends(lengths, seqs)
    half = weights[0].shape[1]
    inner = heads * HEAD
    rows = run * block
    for ref, (k, j, start) in zip(pieces, layout):
        for b in range(ref.shape[0] // block):
            at = (r ^ k) * count + place[k * count + start + b]
            x_ref[rows_at(at, block), j * half : (j + 1) * half] = ref[b * block : (b + 1) * block, :]
    local_runs = q_ref.shape[1] // rows
    shard_runs = local_runs // grid_rows
    lane = lax.broadcasted_iota(jnp.int32, (rows, HEAD), 1)
    down = lax.div(lax.broadcasted_iota(jnp.int32, (rows, HEAD), 0), block)
    ones_v = jnp.where(lane < 3, 1.0, 0.0)
    tail_k = (lane >= seqs) & (lane < seqs + 3)
    q_bias, v_bias = bias[0:1, :].astype(F32), bias[1:2, :].astype(F32)

    def project(i, mine):
        at = rows_at(i, rows)
        x0, x1 = x_ref[at, :half], x_ref[at, half:]
        first = 0 if mine else inner
        joined = nt(x0, weights[0][first:, :]) + nt(x1, weights[1][first:, :])
        seg = sequence_of(ends, down + i * run)
        key_tail = jnp.where((lane == seg) | tail_k, 1.0, 0.0)
        for h in range(heads):
            left = inner - first + h * HEAD
            value = joined[:, left + inner : left + inner + HEAD] + v_bias[:, h * HEAD : (h + 1) * HEAD]
            k_ref[h, at, :] = jnp.concatenate([joined[:, left : left + HEAD], key_tail], axis=1).astype(BF)
            v_ref[h, at, :] = jnp.concatenate([value, ones_v], axis=1).astype(BF)
        return at, joined, seg

    def pair(i, carry):
        project(2 * i + 1 - c, False)
        at, joined, seg = project(2 * i + c, True)
        here = rows_at(i, rows)
        query_tail = jnp.where((lane < seqs) & (lane != seg), OFF, 0.0)
        for h in range(heads):
            query = joined[:, h * HEAD : (h + 1) * HEAD] + q_bias[:, h * HEAD : (h + 1) * HEAD]
            query = query.astype(BF).astype(F32) * (HEAD**-0.5)
            q_ref[h, here, :] = jnp.concatenate([query, query_tail], axis=1).astype(BF)
        xq_ref[here, :] = x_ref[at, :]
        return carry

    lax.fori_loop(0, local_runs, pair, jnp.int32(0))
    own_ref[...] = xq_ref[rows_at(r, rows * shard_runs), :]
    wide = score_ref.shape[3]
    lane_q = lax.broadcasted_iota(jnp.int32, (rows, LANES), 1)

    def one_run(i, carry):
        steps, key_rows = key_steps(ends, i * 2 * run + c * run, run, block, wide, k_ref.shape[1])
        here = rows_at(i, rows)
        peak_ref[...] = jnp.full_like(peak_ref, -3e38)

        def score(j, state):
            for h in range(heads):
                scores = nt(q_ref[h, here, :], k_ref[h, key_rows(j), :])
                score_ref[h, j] = scores
                peak = peak_ref[h]
                for t in range(wide // LANES):
                    peak = jnp.maximum(peak, scores[:, t * LANES : (t + 1) * LANES])
                peak_ref[h] = peak
            return state

        lax.fori_loop(0, steps, score, jnp.int32(0))
        tops = [jnp.max(peak_ref[h], axis=1, keepdims=True) for h in range(heads)]
        for h in range(heads):
            peak_ref[h] = jnp.broadcast_to(tops[h], (rows, LANES))
        acc_ref[...] = jnp.zeros_like(acc_ref)

        def mix(j, state):
            for h in range(heads):
                peak = jnp.concatenate([peak_ref[h]] * (wide // LANES), axis=1)
                part = jnp.exp(score_ref[h, j] - peak).astype(BF)
                acc_ref[h] += nn(part, v_ref[h, key_rows(j), :])
            return state

        lax.fori_loop(0, steps, mix, jnp.int32(0))
        for h in range(heads):
            acc = acc_ref[h]
            total = acc[:, HEAD : HEAD + 1]
            o_ref[h, here, :] = (acc[:, :HEAD] / total).astype(BF)
            kept = q_ref[h, here, :].astype(F32)
            for t, term in enumerate(thirds(tops[h] + jnp.log(total))):
                kept = jnp.where(lane_q == HEAD + seqs + t, -term, kept)
            q_ref[h, here, :] = kept.astype(BF)
        return carry

    lax.fori_loop(0, local_runs, one_run, jnp.int32(0))
    for k in range(grid_rows):
        cells = [
            o_ref[h, rows_at((r ^ k) * shard_runs + part, rows), :] for part in range(shard_runs) for h in range(heads)
        ]
        mixed[k][...] = jnp.concatenate(cells, axis=1)


def attend_back_kernel(
    grid_rows, heads_all, start, seqs, run, block, where, lengths, q_ref, k_ref, v_ref, o_ref, *refs
):
    grads = refs[:grid_rows]
    dq_ref, own_ref, other_ref, do_ref, query_acc, key_acc, value_acc = refs[grid_rows:]
    r, c = where[1], where[2]
    heads = q_ref.shape[0]
    ends = sequence_ends(lengths, seqs)
    rows = run * block
    wide = 2 * rows
    local_runs = q_ref.shape[1] // rows
    shard_runs = local_runs // grid_rows
    lane = lax.broadcasted_iota(jnp.int32, (rows, HEAD), 1)
    for k in range(grid_rows):
        for part in range(shard_runs):
            at = rows_at((r ^ k) * shard_runs + part, rows)
            for h in range(heads):
                left = (part * heads_all + start + h) * HEAD
                grad = grads[k][:, left : left + HEAD].astype(F32)
                centre = jnp.sum(grad * o_ref[h, at, :].astype(F32), axis=1, keepdims=True)
                tail = jnp.zeros((rows, HEAD), F32)
                for t, term in enumerate(thirds(centre)):
                    tail = jnp.where(lane == t, -term, tail)
                do_ref[h, at, :] = jnp.concatenate([grad, tail], axis=1).astype(BF)
    key_acc[...] = jnp.zeros_like(key_acc)
    value_acc[...] = jnp.zeros_like(value_acc)

    def one_run(i, carry):
        steps, key_rows = key_steps(ends, i * 2 * run + c * run, run, block, wide, k_ref.shape[1])
        here = rows_at(i, rows)
        query_acc[...] = jnp.zeros_like(query_acc)

        def keys(j, state):
            at = key_rows(j)
            for h in range(heads):
                query, grad = q_ref[h, here, :], do_ref[h, here, :]
                key = k_ref[h, at, :]
                shares = jnp.exp(nt(key, query))
                score_grads = (shares * nt(v_ref[h, at, :], grad)).astype(BF)
                value_acc[h, at, :] += nn(shares.astype(BF), grad)
                key_acc[h, at, :] += nn(score_grads, query)
                query_acc[h] += tn(score_grads, key)
            return state

        lax.fori_loop(0, steps, keys, jnp.int32(0))
        for h in range(heads):
            dq_ref[h, here, :] = (query_acc[h, :, :HEAD] * (HEAD**-0.5)).astype(BF)
        return carry

    lax.fori_loop(0, local_runs, one_run, jnp.int32(0))

    def pair(i, carry):
        here = rows_at(i, rows)
        for h in range(heads):
            at = rows_at(2 * i + c, rows)
            own_ref[h, here, :] = jnp.concatenate([key_acc[h, at, :HEAD], value_acc[h, at, :HEAD]], axis=1)
            at = rows_at(2 * i + 1 - c, rows)
            other = jnp.concatenate([key_acc[h, at, :HEAD], value_acc[h, at, :HEAD]], axis=1)
            other_ref[h, here, :] = other.astype(BF)
        return carry

    lax.fori_loop(0, local_runs, pair, jnp.int32(0))


def join_kernel(grid_rows, where, dq_ref, own_ref, got_ref, *refs):
    pieces, joined = refs[:grid_rows], refs[grid_rows]
    r = where[1]
    heads, rows = dq_ref.shape[0], pieces[0].shape[0]
    shard_runs = pieces[0].shape[1] // joined.shape[1]
    for k in range(grid_rows):
        cells = []
        for part in range(shard_runs):
            at = rows_at((r ^ k) * shard_runs + part, rows)
            both = [(own_ref[h, at, :] + got_ref[h, at, :].astype(F32)).astype(BF) for h in range(heads)]
            mine = [dq_ref[h, at, :] for h in range(heads)]
            mine += [b[:, :HEAD] for b in both] + [b[:, HEAD:] for b in both]
            joined[at, :] = jnp.concatenate(mine, axis=1)
            cells += mine
        pieces[k][...] = jnp.concatenate(cells, axis=1)


def project_in_grad_kernel(parts, heads, *refs):
    joined, (xq, own, other) = refs[:-3], refs[-3:]
    half = own.shape[1]
    wide = 3 * heads * HEAD
    totals = [[], [], []]
    for (start, number), part in zip(parts, joined):
        span = number * HEAD
        total = jnp.sum(part[...].astype(F32), axis=0, keepdims=True)
        for out, lanes in ((own, slice(0, half)), (other, slice(half, 2 * half))):
            grad = tn(part[...], xq[:, lanes]).astype(BF)
            for i in range(3):
                top = (i * heads + start) * HEAD
                out[top : top + span, :] = grad[i * span : (i + 1) * span, :]
        for i in range(3):
            totals[i].append(total[:, i * span : (i + 1) * span])
    total = jnp.concatenate([*totals[0], *totals[1], *totals[2], jnp.zeros((1, 2 * half - wide), F32)], axis=1)
    below = own.shape[0] - wide
    sums = jnp.concatenate([total[:, :half], total[:, half:], jnp.zeros((below - 2, half), F32)], axis=0).astype(BF)
    own[wide:, :] = sums
    other[wide:, :] = sums


def middle_kernel(plan, grid_rows, where, *refs):
    at = 0

    def take(n):
        nonlocal at
        got = refs[at : at + n]
        at += n
        return got

    r, c = where[1], where[2]
    mixed = take(grid_rows)
    (x_ref,) = take(1)
    dy = take(2)
    first = take(2 * grid_rows)
    (gathered,) = take(1)
    second = [gathered.at[(r ^ k) * 2 + (c ^ j)] for k in range(grid_rows) for j in range(2)]
    outs = list(take(1))
    (grad_one_ref,) = take(1)
    mixed_grad = take(grid_rows)
    first_grad, second_grad = take(2), take(2)
    act_ref, up_grad_ref, hidden_ref, down_grad_ref, attn_grad_ref, slope_ref, small = take(7)
    own_rows, half = dy[0].shape
    outs.append(second_grad[1].at[second_grad[1].shape[0] - own_rows :])
    width = 2 * half
    inner = mixed[0].shape[1] // 2
    rows = mixed[0].shape[0]
    part_hidden = first[0].shape[1]
    small[...] = jnp.zeros_like(small)

    def vector(index):
        row = plan["vectors"] + index
        return jnp.concatenate([second[0][row : row + 1, :], second[1][row : row + 1, :]], axis=1).astype(F32)

    output_bias, first_gain, first_shift, down_bias, second_gain, second_shift = (vector(i) for i in range(6))

    def mean(v):
        return jnp.sum(v, axis=1, keepdims=True) / width

    def norm(v):
        centred = v - mean(v)
        inverse = lax.rsqrt(mean(centred * centred) + EPSILON)
        return centred * inverse, inverse

    def norm_back(v, normed, inverse):
        return inverse * (v - mean(v) - normed * mean(v * normed))

    def total(v):
        return jnp.sum(v, axis=0, keepdims=True)

    def keep(row, v):
        small[row : row + 1, : v.shape[1]] += v

    for part in range(2):
        span = slice(part * rows, (part + 1) * rows)
        lanes = slice(part * inner, (part + 1) * inner)
        parts = []
        for j in range(2):
            parts.append(sum(nn(mixed[k][:, lanes], second[2 * k + j][plan["out"], :]) for k in range(grid_rows)))
        attention = jnp.concatenate(parts, axis=1) + output_bias
        normed_one, inverse_one = norm(x_ref[span, :].astype(F32) + attention)
        hidden = normed_one * first_gain + first_shift
        low = hidden.astype(BF)
        hidden_ref[span, :] = low
        downs = [jnp.zeros((rows, half), F32), jnp.zeros((rows, half), F32)]
        for k in range(grid_rows):
            cols = slice(k * part_hidden, (k + 1) * part_hidden)
            upward = nn(low[:, :half], first[2 * k][...]) + nn(low[:, half:], first[2 * k + 1][...])
            bias = [second[2 * k][plan["up_bias"] + u : plan["up_bias"] + u + 1, :] for u in range(part_hidden // half)]
            upward = upward + jnp.concatenate(bias, axis=1).astype(F32)
            bell = (1.0 + lax.erf(upward * (2.0**-0.5))) * 0.5
            slope_ref[:, cols] = bell + upward * jnp.exp(upward * upward * -0.5) * 0.3989422804014327
            act = (upward * bell).astype(BF)
            act_ref[span, cols] = act
            for j in range(2):
                downs[j] = downs[j] + nn(act, second[2 * k + j][plan["down"], :])
        downward = jnp.concatenate(downs, axis=1) + down_bias
        normed_two, inverse_two = norm(hidden + downward)
        final = (normed_two * second_gain + second_shift).astype(BF)
        outs[0][span, :] = final[:, :half]
        outs[1][span, :] = final[:, half:]
        grad_out = jnp.concatenate([dy[0][span, :], dy[1][span, :]], axis=1).astype(F32)
        keep(0, total(grad_out * normed_two))
        keep(1, total(grad_out))
        grad_two = norm_back(grad_out * second_gain, normed_two, inverse_two)
        down_grad = grad_two.astype(BF)
        down_grad_ref[span, :] = down_grad
        keep(4, total(down_grad.astype(F32)))
        grads = [grad_two[:, :half], grad_two[:, half:]]
        for k in range(grid_rows):
            cols = slice(k * part_hidden, (k + 1) * part_hidden)
            act_grad = nt(down_grad[:, :half], second[2 * k][plan["down"], :]) + nt(
                down_grad[:, half:], second[2 * k + 1][plan["down"], :]
            )
            up_grad = (act_grad * slope_ref[:, cols]).astype(BF)
            up_grad_ref[span, cols] = up_grad
            keep(8 + k, total(up_grad.astype(F32)))
            for j in range(2):
                grads[j] = grads[j] + nt(up_grad, first[2 * k + j][...])
        grad_hidden = jnp.concatenate(grads, axis=1)
        keep(2, total(grad_hidden * normed_one))
        keep(3, total(grad_hidden))
        grad_one = norm_back(grad_hidden * first_gain, normed_one, inverse_one)
        grad_one_ref[span, :] = grad_one
        attn_grad = grad_one.astype(BF)
        attn_grad_ref[span, :] = attn_grad
        keep(5, total(attn_grad.astype(F32)))
        for k in range(grid_rows):
            back = nt(attn_grad[:, :half], second[2 * k][plan["out"], :]) + nt(
                attn_grad[:, half:], second[2 * k + 1][plan["out"], :]
            )
            mixed_grad[k][:, lanes] = back.astype(BF)

    for j in range(2):
        side = slice(j * half, (j + 1) * half)
        for place, k in enumerate(plan["second_order"]):
            cols = slice(k * part_hidden, (k + 1) * part_hidden)
            grad = second_grad[j].at[place * plan["rows"] : (place + 1) * plan["rows"]]
            grad[plan["down"], :] = tn(act_ref[:, cols], down_grad_ref[:, side]).astype(BF)
            back = tn(mixed[k][:, :inner], attn_grad_ref[:rows, side])
            back = back + tn(mixed[k][:, inner:], attn_grad_ref[rows:, side])
            grad[plan["out"], :] = back.astype(BF)
            sums = [small[:6, side]] + [small[8 + k : 9 + k, u * half : (u + 1) * half] for u in range(part_hidden // half)]
            sums += [jnp.zeros((32 - 6 - part_hidden // half, half), F32)]
            grad[plan["sums"], :] = jnp.concatenate(sums, axis=0).astype(BF)
        for place, k in enumerate(plan["first_order"]):
            cols = slice(k * part_hidden, (k + 1) * part_hidden)
            first_grad[j][place, :, :] = tn(hidden_ref[:, side], up_grad_ref[:, cols]).astype(BF)


def input_grad_kernel(grid_rows, parts, where, *refs):
    pieces = [refs[i * grid_rows : (i + 1) * grid_rows] for i in range(parts)]
    weight, grad_one, own, other = refs[parts * grid_rows :]
    r, c = where[1], where[2]
    half = own.shape[1]
    rows = pieces[0][0].shape[0]
    for run in range(2):
        span = slice(run * rows, (run + 1) * rows)
        for j, out in enumerate((own, other)):
            total = grad_one[span, j * half : (j + 1) * half]
            for k in range(grid_rows):
                top = 0
                for part in pieces:
                    wide = part[k].shape[1] // 2
                    held = weight[(r ^ k) * 2 + (c ^ j), top : top + wide, :]
                    total = total + nn(part[k][:, run * wide : (run + 1) * wide], held)
                    top += wide
            out[span, :] = total.astype(BF)


def shift(array, axis, to):
    return lax.ppermute(array, axis, [(i, to(i)) for i in range(lax.axis_size(axis))])


def to_row(array, k):
    return shift(array, "row", lambda i: i ^ k)


def to_col(array):
    return shift(array, "col", lambda i: 1 - i)


def after(array, *earlier):
    return lax.optimization_barrier((array, *earlier))[0]


def gather_near(array):
    return to_row(array, 1), to_row(array, 2)


def gather_row(array, near, side, cut):
    got = [(0, 0, array), (1, 0, near), (2, 0, side), (3, 0, to_row(near[:cut], 2))]
    return got + ([(3, cut, to_row(side[cut:], 1))] if cut < array.shape[0] else [])


def after_all(arrays, *earlier):
    return lax.optimization_barrier((*arrays, *earlier))[: len(arrays)]


def add(*arrays):
    return sum(a.astype(F32) for a in arrays).astype(BF)


def reduce_first(own, got):
    return add(own[2:], got[2:])


def reduce_groups(array, group, second=(), third=()):
    if lax.axis_size("tok") != 4:
        return lax.psum(array, "tok")
    side = (group ^ (group >> 1)) & 1
    middle = array.shape[0] // 2
    low, high = array[:middle], array[middle:]
    half = add(jnp.where(side == 0, low, high), shift(jnp.where(side == 0, high, low), "tok", lambda i: i ^ 1))
    half = after(half, *second)
    half = add(after(half, *third), shift(half, "tok", lambda i: i ^ 3))
    rest = shift(half, "tok", lambda i: i ^ 1)
    return jnp.concatenate([jnp.where(side == 0, half, rest), jnp.where(side == 0, rest, half)], axis=0)


def local(
    tokens,
    cotangent,
    lengths,
    dealing,
    project_in,
    project_bias,
    project_out,
    output_bias,
    first_gain,
    first_shift,
    up_weight,
    up_bias,
    down_weight,
    down_bias,
    second_gain,
    second_shift,
):
    groups, grid_rows = lax.axis_size("tok"), lax.axis_size("row")
    group, row, col = lax.axis_index("tok"), lax.axis_index("row"), lax.axis_index("col")
    where = jnp.stack([group, row, col]).astype(jnp.int32)
    shard_rows, half = tokens.shape
    width = 2 * half
    count = dealing.shape[0] // (groups * grid_rows)
    block = shard_rows // count
    sizes = (groups, grid_rows, count, block)
    seqs = lengths.shape[1]
    inner = project_bias.shape[1]
    heads = inner // HEAD
    hidden_part = up_weight.shape[1]
    run = count // 4
    rows = run * block
    own_rows = shard_rows // 2
    half_rows = own_rows * grid_rows
    wide = 3 * inner
    per_pair = count // groups
    piece = (per_pair * block, half)
    shard = (shard_rows, half)
    both = pltpu.VMEM(shard, BF)

    def exchange(pieces):
        return [shift(p, "tok", lambda i, d=d: (i + d) % groups) if d else p for d, p in enumerate(pieces)]

    joined_weight = project_in.transpose(1, 2, 0).reshape(wide, half)
    out_rows = slice(hidden_part, hidden_part + inner)
    plan = {
        "down": slice(0, hidden_part),
        "out": out_rows,
        "vectors": out_rows.stop,
        "up_bias": out_rows.stop + 6,
        "sums": slice(out_rows.stop, out_rows.stop + 32),
        "rows": out_rows.stop + 32,
        "first_order": (0, 2, 1, 3),
        "second_order": (0, 1, 2, 3),
    }

    *sent, table = call(
        partial(send_kernel, sizes), [(piece, BF)] * groups + [((count + 8,), jnp.int32)], "ssv",
        out_spaces="v" * groups + "s",
    )(dealing, where, tokens)
    (place,) = call(partial(place_kernel, sizes), [((grid_rows * count,), jnp.int32)], "ss", [pltpu.SMEM((groups,), jnp.int32)], "s", 2)(
        dealing, where
    )
    got = exchange(sent)
    vectors = [output_bias, first_gain, first_shift, down_bias, second_gain, second_shift, up_bias]
    vectors = after(jnp.concatenate(vectors), *got).reshape(8, half)
    second_weights = jnp.concatenate(
        [after(down_weight, *got), after(project_out, *got), jnp.pad(vectors, ((0, 8), (0, 0)))], axis=0
    )
    first_near = gather_near(up_weight)
    chunk = jnp.concatenate(after_all(got, place, *first_near), axis=0)
    chunk_near = gather_near(chunk)
    dy_sent = call(partial(send_again_kernel, sizes), [(piece, BF)] * groups, "sv")(table, after(cotangent, *got))
    dy_got = exchange(dy_sent)
    chunk_near = after_all(chunk_near, *dy_got)
    layout, pieces = [], []
    parts = gather_row(chunk, *chunk_near, shard_rows // 2)
    for k, top, part in parts:
        layout += [(k, 0, top // block), (k, 1, top // block)]
        pieces += [part, to_col(part)]
    far = [part for k, _, part in parts if k == 3]
    second_all = lax.all_gather(after(second_weights, *chunk_near), ("row", "col"))
    first_row = after_all((up_weight, *first_near), *chunk_near)
    first_all = [part for weight in first_row for part in (weight, to_col(weight))]
    pieces[0] = after(pieces[0], *first_all)
    first_far = to_row(after(up_weight, *far), 3)
    wide_keys = 2 * rows
    q, k, v, mixed_own, xq, x_own, *mixed = call(
        partial(attend_kernel, sizes, layout, heads, seqs, run),
        [
            ((heads, half_rows, LANES), BF),
            ((heads, 2 * half_rows, LANES), BF),
            ((heads, 2 * half_rows, LANES), BF),
            ((heads, half_rows, HEAD), BF),
            ((half_rows, width), BF),
            ((own_rows, width), BF),
        ]
        + [((rows, 2 * inner), BF)] * grid_rows,
        "sss" + "v" * (len(pieces) + 3),
        [
            pltpu.VMEM((2 * half_rows, width), BF),
            pltpu.VMEM((heads, 2 * half_rows // wide_keys, rows, wide_keys), F32),
            pltpu.VMEM((heads, rows, LANES), F32),
            pltpu.VMEM((heads, rows, LANES), F32),
        ],
        us=47,
    )(place, where, lengths, *pieces, joined_weight, to_col(joined_weight), project_bias)

    mixed = after_all(mixed, first_far)
    dy_got[0] = after(dy_got[0], mixed[0])
    first_far = after(first_far, mixed[0])
    first_all += [first_far, to_col(first_far)]
    dy_own, dy_other = call(
        partial(arrive_kernel, sizes, run), [((own_rows, half), BF)] * 2, "ss" + "v" * groups, [both]
    )(place, where, *dy_got)
    dy = [dy_own, to_col(dy_other)]

    def leave(own, other):
        return call(partial(return_kernel, sizes, run), [(piece, BF)] * groups, "ssvv", [both])(place, where, own, other)

    def come_back(pieces):
        return call(partial(final_kernel, sizes), [(shard, BF)], "s" + "v" * groups)(table, *pieces)[0]

    mixed_got = [to_row(m, i) if i else m for i, m in enumerate(mixed)]
    parts = ((0, heads - 1), (heads - 1, 1))
    held = [(i * heads + start) * HEAD for start, _ in parts for i in range(3)]
    spans = [number * HEAD for _, number in parts for _ in range(3)]
    split = jnp.concatenate([joined_weight[top : top + span] for top, span in zip(held, spans)], axis=0)
    joined_all = lax.all_gather(after(split, mixed[0]), ("row", "col"))
    hidden_all = grid_rows * hidden_part
    second_rows = plan["rows"]
    out0, grad_one, *rest = call(
        partial(middle_kernel, plan, grid_rows),
        [((own_rows, half), BF), ((own_rows, width), F32)]
        + [((rows, 2 * inner), BF)] * grid_rows
        + [((grid_rows, half, hidden_part), BF)] * 2
        + [((grid_rows * second_rows, half), BF), ((grid_rows * second_rows + own_rows, half), BF)],
        "s" + "v" * (grid_rows + 3 + 2 * grid_rows + 1),
        [
            pltpu.VMEM((own_rows, hidden_all), BF),
            pltpu.VMEM((own_rows, hidden_all), BF),
            pltpu.VMEM((own_rows, width), BF),
            pltpu.VMEM((own_rows, width), BF),
            pltpu.VMEM((own_rows, width), BF),
            pltpu.VMEM((rows, hidden_all), F32),
            pltpu.VMEM((16, width), F32),
        ],
        us=42,
    )(where, *mixed_got, x_own, *dy, *first_all, second_all)
    mixed_grad = rest[:grid_rows]
    first_own, first_other, second_own, second_other = rest[grid_rows:]
    mixed_grad_got = [to_row(m, i) if i else m for i, m in enumerate(mixed_grad)]
    first_got, second_got = to_col(first_other), to_col(second_other)
    out_pieces = leave(out0, second_got)
    first_leaving = add(first_own[2:], first_got[2:])
    second_cut = [slice(i * second_rows, (i + 1) * second_rows) for i in range(grid_rows)]
    second_far = slice(2 * second_rows, 4 * second_rows)
    second_leaving = add(second_own[second_far], second_got[second_far])
    first_leaving, second_leaving, *out_pieces = after_all((first_leaving, second_leaving, *out_pieces), *mixed_grad_got)
    first_came, second_came = to_row(first_leaving, 1), to_row(second_leaving, 2)
    out_got = exchange(out_pieces)
    mixed_grad_got[0] = after(mixed_grad_got[0], first_leaving, second_leaving, *out_pieces)

    def back(start, number, grads):
        held = {
            2: ((number, half_rows, LANES), start // number),
            3: ((number, 2 * half_rows, LANES), start // number),
            4: ((number, 2 * half_rows, LANES), start // number),
            5: ((number, half_rows, HEAD), start // number),
        }
        return call(
            partial(attend_back_kernel, grid_rows, heads, start, seqs, run, block),
            [
                ((number, half_rows, HEAD), BF),
                ((number, half_rows, LANES), F32),
                ((number, half_rows, LANES), BF),
            ],
            "ss" + "v" * (4 + grid_rows),
            [
                pltpu.VMEM((number, half_rows, LANES), BF),
                pltpu.VMEM((number, rows, LANES), F32),
                pltpu.VMEM((number, 2 * half_rows, LANES), F32),
                pltpu.VMEM((number, 2 * half_rows, LANES), F32),
            ],
            us=16 * number,
            blocks=held,
        )(where, lengths, q, k, v, mixed_own, *grads)

    def join(dq, own, got):
        number = dq.shape[0]
        *pieces, joined = call(
            partial(join_kernel, grid_rows),
            [((rows, 2 * number * 3 * HEAD), BF)] * grid_rows + [((half_rows, number * 3 * HEAD), BF)],
            "svvv",
            us=2 * number,
        )(where, dq, own, got)
        return [to_row(m, i) if i else m for i, m in enumerate(pieces)], pieces, joined

    dq, kv_own, kv_other = back(0, heads - 1, mixed_grad_got)
    kv_other = after(kv_other, first_came, second_came, *out_got)
    kv_got = to_col(kv_other)
    first_own, second_own, out_got[0] = after_all((first_own, second_own, out_got[0]), dq)
    first_parting = add(first_own[1], first_got[1], first_came[1])
    second_parting = add(second_own[second_cut[1]], second_got[second_cut[1]], second_came[second_rows:])
    first_last, second_last = to_row(first_parting, 2), to_row(second_parting, 1)
    joined_got, leaving, joined = join(dq, kv_own, kv_got)
    mixed_grad_got[0] = after(mixed_grad_got[0], first_parting, second_parting, *leaving)
    dq, kv_own, kv_other = back(heads - 1, 1, mixed_grad_got)
    kv_other = after(kv_other, first_last, second_last, *joined_got)
    first_own, second_own, out_got[0] = after_all((first_own, second_own, out_got[0]), dq)
    first_sum = add(first_own[0], first_got[0], first_came[0], first_last)
    second_sum = add(second_own[second_cut[0]], second_got[second_cut[0]], second_came[:second_rows], second_last)
    kv_got = after(to_col(kv_other), first_sum, second_sum)
    last_got, leaving, last_joined = join(dq, kv_own, kv_got)
    output = come_back(out_got)
    in_own, in_other = call(partial(project_in_grad_kernel, parts, heads), [((wide + 32, half), BF)] * 2, "vvv", us=6)(joined, last_joined, xq)
    in_got = to_col(in_other)
    last_got[0] = after(last_got[0], in_own)
    dx_own, dx_other = call(
        partial(input_grad_kernel, grid_rows, 2), [((own_rows, half), BF)] * 2, "s" + "v" * (2 * grid_rows + 2), us=7
    )(where, *joined_got, *last_got, joined_all, grad_one)
    dx_pieces = leave(dx_own, to_col(dx_other))
    first_sum = reduce_groups(first_sum, group, (last_joined,), dx_pieces)
    second_sum = reduce_groups(second_sum, group, (last_joined,), dx_pieces)
    dx_got = exchange(dx_pieces)
    input_grad = come_back(dx_got)
    in_sum = reduce_groups(add(in_own, in_got), group, dx_pieces)

    project_in_grad = in_sum[:wide].reshape(3, inner, half).transpose(2, 0, 1)
    sums = in_sum[wide : wide + 2].reshape(2 * half)
    sums = [sums[:inner], sums[2 * inner : 3 * inner]]
    tail = second_sum[plan["sums"]].astype(F32)
    return (
        output,
        input_grad,
        project_in_grad.astype(F32),
        jnp.stack(sums).astype(F32),
        second_sum[out_rows].astype(F32),
        tail[5],
        tail[2],
        tail[3],
        first_sum.astype(F32),
        tail[6:8].reshape(hidden_part),
        second_sum[:hidden_part].astype(F32),
        tail[4],
        tail[0],
        tail[1],
    )


def solution(mesh):
    stream, grid = P(("tok", "row"), "col"), P("row", "col")
    joined, mids, cols = P("col", None, "row"), P("col", "row"), P("col")
    in_specs = (
        stream, stream, P("tok", None), P(), joined, P(None, "row"), grid, cols,
        cols, cols, mids, P("row"), grid, cols, cols, cols,
    )
    out_specs = (
        stream, stream, joined, P(None, "row"), grid, cols,
        cols, cols, mids, P("row"), grid, cols, cols, cols,
    )
    return jax.shard_map(local, mesh=mesh, in_specs=in_specs, out_specs=out_specs, check_vma=False)
```
